1024 devices in a mesh: row: 16 (over x, z_hi, core), col: 64 (over y, z_lo).
Axes of the slice: x: 4, y: 4, z: 32 (z_hi: 2, z_lo: 16; z = z_hi * 16 + z_lo), core: 2. Of those that a mesh axis runs over, the one named last changes fastest.
Arguments:
- images: float32 [4096, 1152], P(('row', 'col')), may hold values from -0.1875 to 0.1875
- texts: float32 [4096, 1152], P(('col', 'row')), may hold values from -0.1875 to 0.1875
- log_temp: float32 [1], replicated, may hold values from 1 to 1.6
- bias: float32 [1], replicated, may hold values from -4 to -2
Outputs:
- image_grad: float32 [4096, 1152], P(('row', 'col'))
- text_grad: float32 [4096, 1152], P(('col', 'row'))
- loss: float32 [], replicated
- temp_grad: float32 [], replicated
- bias_grad: float32 [], replicated
The draws below stay inside these ranges and needn't reach their ends.
All inputs are finite; a program needn't handle non-finite values.
Results may differ from the reference program's by a relative error of at most 0.0041.
Values may be sent and summed in bfloat16 or wider, within the bound.
A program may use at most 32 MiB of HBM per device.

```python
import jax
import jax.numpy as jnp
from jax import lax

D = 1152
IMG_BLOCK = 256
PAIRS = 4096


def levels(own_key, extent, split, smallest, high):
    gain, own = 1.0, jax.random.fold_in(own_key, 6)
    for axis_at, shards_of in split:
        steps = jnp.exp(jax.random.uniform(jax.random.fold_in(own, axis_at), (shards_of,), jnp.float32, smallest / len(split), high / len(split)))
        gain = gain * jnp.repeat(steps, extent[axis_at] // shards_of).reshape([-1 if axis == axis_at else 1 for axis in range(len(extent))])
    return gain


def noise(key, extent, spread, reach, cuts=(), kind=jnp.bfloat16):
    values = jax.random.normal(key, extent, jnp.float32) * spread
    if len(cuts) > 0:
        values = levels(key, extent, cuts, -0.22, 0.18) * values
    return jnp.clip(values, min=-reach, max=reach).astype(kind)


def setup_inputs(seed: int = 0) -> dict:
    key_of = jax.random.split(jax.random.key(seed), 5)
    images = noise(key_of[0], (PAIRS, D), D ** -0.5, 0.1875, ((0, 1024),), jnp.float32)
    texts = noise(key_of[1], (PAIRS, D), D ** -0.5, 0.1875, ((0, 1024),), jnp.float32)
    log_temp = jnp.clip(jax.random.uniform(key_of[2], (1,), jnp.float32, 1.0, 1.6), 1.0, 1.6)
    bias = jnp.clip(jax.random.uniform(key_of[3], (1,), jnp.float32, -4.0, -2.0), -4.0, -2.0)
    return dict(images=images, texts=texts, log_temp=log_temp, bias=bias)


def normalize(values):
    norms = jnp.sqrt(lax.optimization_barrier(jnp.sum(values * values, axis=-1, keepdims=True)) + 1e-06)
    return (values / norms, norms)

def unit_backward(unit, norms, grads):
    along = lax.optimization_barrier(jnp.sum(unit * grads, axis=-1, keepdims=True))
    return (grads - unit * along) / norms

def reference(images, texts, log_temp, bias):
    img_unit, img_norm = normalize(images)
    txt_unit, txt_norm = normalize(texts)
    img_low = img_unit.astype(jnp.bfloat16)
    txt_low = txt_unit.astype(jnp.bfloat16)
    temp = jnp.exp(log_temp[0])
    offset = bias[0]
    count = PAIRS // IMG_BLOCK
    blocks = img_low.reshape(count, IMG_BLOCK, D)
    columns = jnp.arange(PAIRS, dtype=jnp.int32)

    def step(carry, item):
        txt_acc, loss_acc, slope_acc, shift_acc = carry
        index, rows = item
        scores = lax.dot_general(rows, txt_low, (((1,), (1,)), ((), ())), preferred_element_type=jnp.float32)
        logits = temp * scores + offset
        row_ids = index * IMG_BLOCK + jnp.arange(IMG_BLOCK, dtype=jnp.int32)
        label = jnp.where(row_ids[:, None] == columns[None, :], 1.0, -1.0).astype(jnp.float32)
        margin = -label * logits
        dlogit = -label * jax.nn.sigmoid(margin)
        dlogit_low = dlogit.astype(jnp.bfloat16)
        img_part = temp * jnp.dot(dlogit_low, txt_low, preferred_element_type=jnp.float32)
        txt_part = lax.dot_general(dlogit_low, rows, (((0,), (0,)), ((), ())), preferred_element_type=jnp.float32)
        carry = (txt_acc + txt_part, loss_acc + jnp.sum(jax.nn.softplus(margin)), slope_acc + jnp.sum(dlogit * scores), shift_acc + jnp.sum(dlogit))
        return (carry, img_part)
    start = (jnp.zeros((PAIRS, D), jnp.float32), jnp.float32(0.0), jnp.float32(0.0), jnp.float32(0.0))
    final, img_parts = lax.scan(step, start, (jnp.arange(count, dtype=jnp.int32), blocks))
    txt_acc, loss_acc, slope_acc, shift_acc = final
    img_unit_grad = img_parts.reshape(PAIRS, D)
    txt_unit_grad = temp * txt_acc
    image_grad = unit_backward(img_unit, img_norm, img_unit_grad)
    text_grad = unit_backward(txt_unit, txt_norm, txt_unit_grad)
    scale = 1.0 / (float(PAIRS) * float(PAIRS))
    return (image_grad, text_grad, loss_acc * scale, temp * slope_acc * scale, shift_acc * scale)
```

```python
import functools

import jax
import jax.numpy as jnp
from jax import lax
from jax.experimental import pallas as pl
from jax.experimental.pallas import tpu as pltpu
from jax.sharding import PartitionSpec as P

MESH = pl.DeviceIdType.MESH
F32 = jnp.float32
BF16 = jnp.bfloat16

FACTORS = dict(nx=4, nzh=2, nc=2, ny=4, nzl=16, run=8)


def remote(src, dst, send, recv, dev):
    return pltpu.make_async_remote_copy(
        src_ref=src, dst_ref=dst, send_sem=send, recv_sem=recv, device_id=dev, device_id_type=MESH
    )


def kernel(
    nx, nzh, nc, ny, nzl, run,
    images, texts, log_temp, bias,
    image_grad, text_grad, terms,
    unit, norm, img_all, txt_all, img_out, txt_out, img_in, txt_in,
    img_zout, txt_zout, img_zin, txt_zin, sc_yc, sc_x, sc_zr, sc_zs,
    s_iz, r_iz, s_tz, r_tz, s_ix, r_ix, s_ty, r_ty,
    s_bx, r_bx, s_by, r_by, s_bi, r_bi, s_bt, r_bt,
    s_ay, r_ay, s_ax, r_ax, s_ar, r_ar, s_as, r_as,
):
    own, width = images.shape
    cut = nzl // run
    nzs = nzh * cut
    nyc = ny * nc
    row, col = lax.axis_index("row"), lax.axis_index("col")
    x, zh, core = row // (nzh * nc), (row // nc) % nzh, row % nc
    y, zl = col // nzl, col % nzl
    zr, zs, yc = zl % run, zh * cut + zl // run, y * nc + core

    def device(x_, y_, core_, zs_, zr_):
        return ((x_ * nzh + zs_ // cut) * nc + core_, y_ * nzl + (zs_ % cut) * run + zr_)

    def on_zr(k):
        to = lax.rem(zr + k, run)
        return to, device(x, y, core, zs, to)

    def on_zs(k):
        to = lax.rem(zs + k, nzs)
        return to, device(x, y, core, to, zr)

    def on_x(k):
        to = lax.rem(x + k, nx)
        return to, device(to, y, core, zs, zr)

    def on_yc(k):
        to = lax.rem(yc + k, nyc)
        return to, device(x, to // nc, lax.rem(to, nc), zs, zr)

    groups = ((on_zs, nzs), (on_yc, nyc), (on_x, nx), (on_zr, run))
    barrier = pltpu.get_barrier_semaphore()
    for peer, count in groups:
        for k in range(1, count):
            pl.semaphore_signal(barrier, inc=1, device_id=peer(k)[1], device_id_type=MESH)

    temp = jnp.exp(jnp.full((1, 1), log_temp[0], F32))
    offset = bias[0]
    for at, values, slot in ((0, images, img_all.at[x, zr]), (1, texts, txt_all.at[yc, zs])):
        v = values[...]
        n = jnp.sqrt(jnp.sum(v * v, axis=-1, keepdims=True) + 1e-06)
        u = v / n
        norm[at] = n
        unit[at] = u
        slot[...] = u.astype(BF16)

    pl.semaphore_wait(barrier, sum(count - 1 for _, count in groups))
    pending = []

    def spread(peer, count, source, target, send, recv):
        for k in range(1, count):
            to, dev = peer(k)
            copy = remote(source(to), target, send.at[to], recv, dev)
            copy.start()
            pending.append(copy)

    def arrive(peer, count, slot, recv):
        for k in range(1, count):
            to, dev = peer(k)
            remote(slot(to), slot(to), recv.at[to], recv.at[to], dev).wait_recv()

    mine_i, mine_t = img_all.at[x, zr], txt_all.at[yc, zs]
    spread(on_zs, nzs, lambda to: mine_t, mine_t, s_tz, r_tz.at[zs])
    spread(on_zr, run, lambda to: mine_i, mine_i, s_iz, r_iz.at[zr])
    arrive(on_zs, nzs, lambda to: txt_all.at[yc, to], r_tz)
    spread(on_yc, nyc, lambda to: txt_all.at[yc], txt_all.at[yc], s_ty, r_ty.at[yc])
    arrive(on_zr, run, lambda to: img_all.at[x, to], r_iz)
    spread(on_x, nx, lambda to: img_all.at[x], img_all.at[x], s_ix, r_ix.at[x])
    arrive(on_yc, nyc, lambda to: txt_all.at[to], r_ty)
    arrive(on_x, nx, lambda to: img_all.at[to], r_ix)

    n_img, n_txt = nx * run * own, nyc * nzs * own
    img = img_all[...].astype(F32).reshape(n_img, width).astype(BF16)
    txt = txt_all[...].astype(F32).reshape(n_txt, width).astype(BF16)
    scores = lax.dot_general(txt, img, (((1,), (1,)), ((), ())), preferred_element_type=F32)
    at_i = lax.broadcasted_iota(jnp.int32, (1, n_img), 1)
    at_t = lax.broadcasted_iota(jnp.int32, (n_txt, 1), 0)
    i_row, i_col = device(at_i // (run * own), y, core, zs, (at_i // own) % run)
    t_yc = at_t // (nzs * own)
    t_row, t_col = device(x, t_yc // nc, t_yc % nc, (at_t // own) % nzs, zr)
    rows, cols = nx * nzh * nc, ny * nzl
    i_id = (i_row * cols + i_col) * own + at_i % own
    t_id = (t_col * rows + t_row) * own + at_t % own
    same = i_id == t_id
    logits = temp * scores + offset
    margin = jnp.where(same, -logits, logits)
    e = jnp.exp(-jnp.abs(margin))
    sig = jnp.where(margin >= 0, 1.0, e) / (1.0 + e)
    dlogit = jnp.where(same, -sig, sig)
    loss = jnp.maximum(margin, 0.0) + jnp.log1p(e)

    def total(v):
        return jnp.sum(jnp.sum(v, axis=0, keepdims=True), axis=1, keepdims=True)

    lane = lax.broadcasted_iota(jnp.int32, (1, 128), 1)
    sums = jnp.where(
        lane == 0, total(loss), jnp.where(lane == 1, total(dlogit * scores), total(dlogit))
    )
    low = dlogit.astype(BF16)

    sc_yc[yc] = sums
    spread(on_yc, nyc, lambda to: sc_yc.at[yc], sc_yc.at[yc], s_ay, r_ay.at[yc])

    txt_part = jnp.dot(low, img, preferred_element_type=F32)
    txt_out[...] = txt_part.reshape(nyc, nzs, own, width).astype(BF16)
    spread(on_yc, nyc, lambda to: txt_out.at[to], txt_in.at[yc], s_by, r_by.at[yc])
    img_part = lax.dot_general(low, txt, (((0,), (0,)), ((), ())), preferred_element_type=F32)
    img_out[...] = img_part.reshape(nx, run, own, width).astype(BF16)
    spread(on_x, nx, lambda to: img_out.at[to], img_in.at[x], s_bx, r_bx.at[x])

    txt_in[yc] = txt_out[yc]
    img_in[x] = img_out[x]

    arrive(on_yc, nyc, lambda to: sc_yc.at[to], r_ay)
    sc_x[x] = jnp.sum(sc_yc[...], axis=0)
    spread(on_x, nx, lambda to: sc_x.at[x], sc_x.at[x], s_ax, r_ax.at[x])

    arrive(on_yc, nyc, lambda to: txt_in.at[to], r_by)
    txt_zout[...] = jnp.sum(txt_in[...].astype(F32), axis=0).astype(BF16)
    spread(on_zs, nzs, lambda to: txt_zout.at[to], txt_zin.at[zs], s_bt, r_bt.at[zs])
    txt_zin[zs] = txt_zout[zs]

    arrive(on_x, nx, lambda to: sc_x.at[to], r_ax)
    sc_zr[zr] = jnp.sum(sc_x[...], axis=0)
    spread(on_zr, run, lambda to: sc_zr.at[zr], sc_zr.at[zr], s_ar, r_ar.at[zr])

    arrive(on_x, nx, lambda to: img_in.at[to], r_bx)
    img_zout[...] = jnp.sum(img_in[...].astype(F32), axis=0).astype(BF16)
    spread(on_zr, run, lambda to: img_zout.at[to], img_zin.at[zr], s_bi, r_bi.at[zr])
    img_zin[zr] = img_zout[zr]

    arrive(on_zr, run, lambda to: sc_zr.at[to], r_ar)
    sc_zs[zs] = jnp.sum(sc_zr[...], axis=0)
    spread(on_zs, nzs, lambda to: sc_zs.at[zs], sc_zs.at[zs], s_as, r_as.at[zs])

    def finish(at, gathered, out):
        g = temp * jnp.sum(gathered[...].astype(F32), axis=0)
        u = unit[at]
        along = jnp.sum(u * g, axis=-1, keepdims=True)
        out[...] = (g - u * along) / norm[at]

    arrive(on_zs, nzs, lambda to: txt_zin.at[to], r_bt)
    finish(1, txt_zin, text_grad)
    arrive(on_zr, run, lambda to: img_zin.at[to], r_bi)
    finish(0, img_zin, image_grad)

    arrive(on_zs, nzs, lambda to: sc_zs.at[to], r_as)
    pairs = float(rows * cols * own)
    scale = 1.0 / (pairs * pairs)
    result = jnp.sum(sc_zs[...], axis=0) * scale
    terms[...] = jnp.where(lane == 1, temp, 1.0) * result
    for copy in pending:
        copy.wait_send()


def on_device(factors, images, texts, log_temp, bias):
    nx, nzh, nc, ny, nzl, run = (factors[k] for k in ("nx", "nzh", "nc", "ny", "nzl", "run"))
    nzs, nyc = nzh * nzl // run, ny * nc
    own, width = images.shape
    vmem = pl.BlockSpec(memory_space=pltpu.VMEM)
    smem = pl.BlockSpec(memory_space=pltpu.SMEM)

    def low(*lead):
        return pltpu.VMEM(lead + (own, width), BF16)

    def sems(*counts):
        out = []
        for c in counts:
            out += [pltpu.SemaphoreType.DMA((c,)), pltpu.SemaphoreType.DMA((c,))]
        return out

    image_grad, text_grad, terms = pl.pallas_call(
        functools.partial(kernel, nx, nzh, nc, ny, nzl, run),
        out_shape=(
            jax.ShapeDtypeStruct((own, width), F32),
            jax.ShapeDtypeStruct((own, width), F32),
            jax.ShapeDtypeStruct((1, 128), F32),
        ),
        in_specs=[vmem, vmem, smem, smem],
        out_specs=(vmem, vmem, vmem),
        scratch_shapes=[
            pltpu.VMEM((2, own, width), F32),
            pltpu.VMEM((2, own, 1), F32),
            low(nx, run), low(nyc, nzs),
            low(nx, run), low(nyc, nzs), low(nx, run), low(nyc, nzs),
            low(run), low(nzs), low(run), low(nzs),
            pltpu.VMEM((nyc, 1, 128), F32),
            pltpu.VMEM((nx, 1, 128), F32),
            pltpu.VMEM((run, 1, 128), F32),
            pltpu.VMEM((nzs, 1, 128), F32),
        ] + sems(run, nzs, nx, nyc, nx, nyc, run, nzs, nyc, nx, run, nzs),
        compiler_params=pltpu.CompilerParams(
            collective_id=0, has_side_effects=True, vmem_limit_bytes=32 * 1024 * 1024
        ),
    )(images, texts, log_temp, bias)
    return image_grad, text_grad, terms[0, 0], terms[0, 1], terms[0, 2]


def solution(mesh, factors=FACTORS):
    in_specs = (P(("row", "col"), None), P(("col", "row"), None), P(), P())
    out_specs = (P(("row", "col"), None), P(("col", "row"), None), P(), P(), P())
    return jax.shard_map(
        functools.partial(on_device, factors),
        mesh=mesh, in_specs=in_specs, out_specs=out_specs, check_vma=False,
    )
```

```python
import functools

import jax
import jax.numpy as jnp
from jax import lax
from jax.experimental import pallas as pl
from jax.experimental.pallas import tpu as pltpu
from jax.sharding import PartitionSpec as P

MESH = pl.DeviceIdType.MESH
F32 = jnp.float32
BF16 = jnp.bfloat16

FACTORS = dict(
    nx=4, nzh=2, nc=2, ny=4, nzl=16,
    img_to=(9, -8, 8, -7), txt_to=(7, -7, 5, -5, 3, -3, 1, -1),
)


def remote(src, dst, send, recv, dev):
    return pltpu.make_async_remote_copy(
        src_ref=src, dst_ref=dst, send_sem=send, recv_sem=recv, device_id=dev, device_id_type=MESH
    )


def kernel(
    nx, nzh, nc, ny, nzl, img_to, txt_to,
    images, texts, log_temp, bias,
    image_grad, text_grad, terms,
    raw, unit, norm, img_own, txt_own, img_all, txt_all, img_out, txt_out, img_in, txt_in,
    img_zout, txt_zout, img_zin, txt_zin, sc_near, sc_z, load_sem,
    s_iz, r_iz, s_tz, r_tz, s_ix, r_ix, s_ty, r_ty,
    s_bx, r_bx, s_by, r_by, s_bi, r_bi, s_bt, r_bt, s_sn, r_sn, s_sz, r_sz,
):
    own, width = images.shape
    nz, nxc, nq = nzh * nzl, nx * nc, nx * ny * nc
    na, nb = len(img_to), len(txt_to)
    row, col = lax.axis_index("row"), lax.axis_index("col")
    x, zh, core = row // (nzh * nc), (row // nc) % nzh, row % nc
    y, zl = col // nzl, col % nzl
    z, xc, q = zh * nzl + zl, x * nc + core, (x * ny + y) * nc + core

    def device(x_, y_, core_, z_):
        return ((x_ * nzh + z_ // nzl) * nc + core_, y_ * nzl + z_ % nzl)

    def at_z(step):
        return device(x, y, core, lax.rem(z + (step + nz), nz))

    def at_xc(k):
        to = lax.rem(xc + k, nxc)
        return to, device(to // nc, y, lax.rem(to, nc), z)

    def at_y(k):
        to = lax.rem(y + k, ny)
        return to, device(x, to, core, z)

    z_steps = sorted({s % nz for a in img_to + txt_to for s in (a, -a)}, key=lambda s: -min(s, nz - s))
    greeted = [at_z(s) for s in z_steps]
    greeted += [at_y(k)[1] for k in range(1, ny)] + [at_xc(k)[1] for k in range(1, nxc)]
    barrier = pltpu.get_barrier_semaphore()
    for dev in greeted:
        pl.semaphore_signal(barrier, inc=1, device_id=dev, device_id_type=MESH)

    loads = [
        pltpu.make_async_copy(ref, raw.at[at], load_sem.at[at])
        for at, ref in enumerate((images, texts))
    ]
    for load in loads:
        load.start()
    temp = jnp.exp(jnp.full((1, 1), log_temp[0], F32))
    offset = bias[0]
    for at, slot in ((0, img_own), (1, txt_own)):
        loads[at].wait()
        v = raw[at]
        n = jnp.sqrt(jnp.sum(v * v, axis=-1, keepdims=True) + 1e-06)
        u = v / n
        norm[at] = n
        unit[at] = u
        slot[...] = u.astype(BF16)
    pl.semaphore_wait(barrier, len(greeted))

    pending = []

    def send(src, dst, s_sem, r_sem, dev):
        copy = remote(src, dst, s_sem, r_sem, dev)
        copy.start()
        pending.append(copy)

    def arrived(slot, sem):
        remote(slot, slot, sem, sem, at_z(1)).wait_recv()

    trips = [(abs(a), 0, i, a) for i, a in enumerate(img_to)] + [(abs(b), 1, i, b) for i, b in enumerate(txt_to)]
    for _, kind, i, step in sorted(trips, key=lambda t: -t[0]):
        if kind == 0:
            send(img_own, img_all.at[xc, i], s_iz.at[i], r_iz.at[i], at_z(step))
        else:
            send(txt_own, txt_all.at[y, i], s_tz.at[i], r_tz.at[i], at_z(step))
    for i in range(nb):
        arrived(txt_all.at[y, i], r_tz.at[i])
    for k in range(1, ny):
        to, dev = at_y(k)
        send(txt_all.at[y], txt_all.at[y], s_ty.at[to], r_ty.at[y], dev)
    for i in range(na):
        arrived(img_all.at[xc, i], r_iz.at[i])
    for k in range(1, nxc):
        to, dev = at_xc(k)
        send(img_all.at[xc], img_all.at[xc], s_ix.at[to], r_ix.at[xc], dev)
    for k in range(1, ny):
        to, _ = at_y(k)
        arrived(txt_all.at[to], r_ty.at[to])
    for k in range(1, nxc):
        to, _ = at_xc(k)
        arrived(img_all.at[to], r_ix.at[to])

    n_img, n_txt = nxc * na * own, ny * nb * own
    img = img_all[...].astype(F32).reshape(n_img, width).astype(BF16)
    txt = txt_all[...].astype(F32).reshape(n_txt, width).astype(BF16)
    scores = lax.dot_general(txt, img, (((1,), (1,)), ((), ())), preferred_element_type=F32)
    at_i = lax.broadcasted_iota(jnp.int32, (1, n_img), 1)
    at_t = lax.broadcasted_iota(jnp.int32, (n_txt, 1), 0)

    def stepped(steps, index):
        value = jnp.zeros_like(index)
        for i, s in enumerate(steps):
            value = jnp.where(index == i, s, value)
        return value

    i_xc, i_z = at_i // (na * own), (z + nz - stepped(img_to, (at_i // own) % na)) % nz
    t_y, t_z = at_t // (nb * own), (z + nz - stepped(txt_to, (at_t // own) % nb)) % nz
    i_row, i_col = device(i_xc // nc, y, i_xc % nc, i_z)
    t_row, t_col = device(x, t_y, core, t_z)
    rows, cols = nx * nzh * nc, ny * nzl
    i_id = (i_row * cols + i_col) * own + at_i % own
    t_id = (t_col * rows + t_row) * own + at_t % own
    same = i_id == t_id
    logits = temp * scores + offset
    margin = jnp.where(same, -logits, logits)
    e = jnp.exp(-jnp.abs(margin))
    sig = jnp.where(margin >= 0, 1.0, e) / (1.0 + e)
    dlogit = jnp.where(same, -sig, sig)
    loss = jnp.maximum(margin, 0.0) + jnp.log1p(e)

    def total(v):
        return jnp.sum(jnp.sum(v, axis=0, keepdims=True), axis=1, keepdims=True)

    lane = lax.broadcasted_iota(jnp.int32, (1, 128), 1)
    sc_near[q] = jnp.where(
        lane == 0, total(loss), jnp.where(lane == 1, total(dlogit * scores), total(dlogit))
    )
    for k in range(1, nq):
        to = lax.rem(q + k, nq)
        dev = device(to // (ny * nc), (to // nc) % ny, lax.rem(to, nc), z)
        remote(sc_near.at[q], sc_near.at[q], s_sn, r_sn, dev).start()

    low = dlogit.astype(BF16)
    txt_part = jnp.dot(low, img, preferred_element_type=F32)
    txt_out[...] = txt_part.reshape(ny, nb, own, width).astype(BF16)
    for k in range(1, ny):
        to, dev = at_y(k)
        send(txt_out.at[to], txt_in.at[y], s_by.at[to], r_by.at[y], dev)
    img_part = lax.dot_general(low, txt, (((0,), (0,)), ((), ())), preferred_element_type=F32)
    img_out[...] = img_part.reshape(nxc, na, own, width).astype(BF16)
    for k in range(1, nxc):
        to, dev = at_xc(k)
        send(img_out.at[to], img_in.at[xc], s_bx.at[to], r_bx.at[xc], dev)

    remote(sc_near.at[pl.ds(0, nq - 1)], sc_near.at[pl.ds(0, nq - 1)], s_sn, r_sn, at_z(1)).wait_recv()
    sc_z[z] = jnp.sum(sc_near[...], axis=0)
    for k in sorted(range(1, nz), key=lambda s: -min(s, nz - s)):
        remote(sc_z.at[z], sc_z.at[z], s_sz, r_sz, at_z(k)).start()

    acc = txt_out[y].astype(F32)
    for k in range(1, ny):
        to, _ = at_y(k)
        arrived(txt_in.at[to], r_by.at[to])
        acc += txt_in[to].astype(F32)
    txt_zout[...] = acc.astype(BF16)
    for i, b in enumerate(txt_to):
        send(txt_zout.at[i], txt_zin.at[i], s_bt.at[i], r_bt.at[i], at_z(-b))
    acc = img_out[xc].astype(F32)
    for k in range(1, nxc):
        to, _ = at_xc(k)
        arrived(img_in.at[to], r_bx.at[to])
        acc += img_in[to].astype(F32)
    img_zout[...] = acc.astype(BF16)
    for i, a in enumerate(img_to):
        send(img_zout.at[i], img_zin.at[i], s_bi.at[i], r_bi.at[i], at_z(-a))

    def finish(at, gathered, sem, out):
        for i in range(gathered.shape[0]):
            arrived(gathered.at[i], sem.at[i])
        g = temp * jnp.sum(gathered[...].astype(F32), axis=0)
        u = unit[at]
        along = jnp.sum(u * g, axis=-1, keepdims=True)
        out[...] = (g - u * along) / norm[at]

    finish(1, txt_zin, r_bt, text_grad)
    finish(0, img_zin, r_bi, image_grad)

    for copy in pending:
        copy.wait_send()
    rest = sc_near.at[pl.ds(0, nq - 1)]
    remote(rest, rest, s_sn, r_sn, at_z(1)).wait_send()
    rest = sc_z.at[pl.ds(0, nz - 1)]
    remote(rest, rest, s_sz, r_sz, at_z(1)).wait_send()
    remote(rest, rest, s_sz, r_sz, at_z(1)).wait_recv()
    pairs = float(rows * cols * own)
    scale = 1.0 / (pairs * pairs)
    result = jnp.sum(sc_z[...], axis=0) * scale
    terms[...] = jnp.where(lane == 1, temp, 1.0) * result


def on_device(factors, images, texts, log_temp, bias):
    nx, nzh, nc, ny, nzl, img_to, txt_to = (
        factors[k] for k in ("nx", "nzh", "nc", "ny", "nzl", "img_to", "txt_to")
    )
    nxc, na, nb = nx * nc, len(img_to), len(txt_to)
    own, width = images.shape
    vmem = pl.BlockSpec(memory_space=pltpu.VMEM)
    smem = pl.BlockSpec(memory_space=pltpu.SMEM)
    hbm = pl.BlockSpec(memory_space=pl.ANY)

    def low(*lead):
        return pltpu.VMEM(lead + (own, width), BF16)

    def sems(*counts):
        return [pltpu.SemaphoreType.DMA((c,)) for c in counts for _ in range(2)]

    image_grad, text_grad, terms = pl.pallas_call(
        functools.partial(kernel, nx, nzh, nc, ny, nzl, img_to, txt_to),
        out_shape=(
            jax.ShapeDtypeStruct((own, width), F32),
            jax.ShapeDtypeStruct((own, width), F32),
            jax.ShapeDtypeStruct((1, 128), F32),
        ),
        in_specs=[hbm, hbm, smem, smem],
        out_specs=(vmem, vmem, vmem),
        scratch_shapes=[
            pltpu.VMEM((2, own, width), F32),
            pltpu.VMEM((2, own, width), F32),
            pltpu.VMEM((2, own, 1), F32),
            low(), low(),
            low(nxc, na), low(ny, nb),
            low(nxc, na), low(ny, nb), low(nxc, na), low(ny, nb),
            low(na), low(nb), low(na), low(nb),
            pltpu.VMEM((nx * ny * nc, 1, 128), F32),
            pltpu.VMEM((nzh * nzl, 1, 128), F32),
            pltpu.SemaphoreType.DMA((2,)),
        ] + sems(na, nb, nxc, ny, nxc, ny, na, nb) + [pltpu.SemaphoreType.DMA] * 4,
        compiler_params=pltpu.CompilerParams(
            collective_id=0, has_side_effects=True, vmem_limit_bytes=48 * 1024 * 1024
        ),
    )(images, texts, log_temp, bias)
    return image_grad, text_grad, terms[0, 0], terms[0, 1], terms[0, 2]


def solution(mesh, factors=FACTORS):
    in_specs = (P(("row", "col"), None), P(("col", "row"), None), P(), P())
    out_specs = (P(("row", "col"), None), P(("col", "row"), None), P(), P(), P())
    return jax.shard_map(
        functools.partial(on_device, factors),
        mesh=mesh, in_specs=in_specs, out_specs=out_specs, check_vma=False,
    )
```

```python
import functools

import jax
import jax.numpy as jnp
from jax import lax
from jax.experimental import pallas as pl
from jax.experimental.pallas import tpu as pltpu
from jax.sharding import PartitionSpec as P

MESH = pl.DeviceIdType.MESH
F32 = jnp.float32
BF16 = jnp.bfloat16

FACTORS = dict(
    nx=4, nzh=2, nc=2, ny=4, nzl=16,
    img_steps=(4, -4), img_next=((5, 4), (-4, -3)), txt_steps=(4, -4), txt_next=(1, -1, 3, -3),
    greet=(4, 3, 1), reach=(13, 12), relay=8,
)


def remote(src, dst, send, recv, dev):
    return pltpu.make_async_remote_copy(
        src_ref=src, dst_ref=dst, send_sem=send, recv_sem=recv, device_id=dev, device_id_type=MESH
    )


def kernel(
    nx, nzh, nc, ny, nzl, img_steps, img_next, txt_steps, txt_next, greet, reach, relay,
    images, texts, log_temp, bias,
    image_grad, text_grad, terms,
    raw, unit, norm, img_own, txt_own, img_way, txt_way, img_all, txt_all, img_out, txt_out, img_in, txt_in,
    img_zout, txt_zout, img_zin, txt_zin, sc_near, sc_z, load_sem,
    s_iw, r_iw, s_tw, r_tw, s_iz, r_iz, s_tz, r_tz, s_ix, r_ix, s_ty, r_ty,
    s_bx, r_bx, s_by, r_by, s_bi, r_bi, s_bt, r_bt, s_sn, r_sn, s_sz, r_sz, r_relay,
):
    own, width = images.shape
    nz, nxc, nq = nzh * nzl, nx * nc, nx * ny * nc
    img_to = [a + b for a, after in zip(img_steps, img_next) for b in after]
    txt_to = [a + b for b in txt_next for a in txt_steps]
    na, nb = len(img_to), len(txt_to)
    row, col = lax.axis_index("row"), lax.axis_index("col")
    x, zh, core = row // (nzh * nc), (row // nc) % nzh, row % nc
    y, zl = col // nzl, col % nzl
    z, xc, q = zh * nzl + zl, x * nc + core, (x * ny + y) * nc + core

    def device(x_, y_, core_, z_):
        return ((x_ * nzh + z_ // nzl) * nc + core_, y_ * nzl + z_ % nzl)

    def at_z(step):
        return device(x, y, core, lax.rem(z + (step + nz), nz))

    def at_xc(k):
        to = lax.rem(xc + k, nxc)
        return to, device(to // nc, y, lax.rem(to, nc), z)

    def at_y(k):
        to = lax.rem(y + k, ny)
        return to, device(x, to, core, z)

    z_steps = sorted({s % nz for a in greet for s in (a, -a)}, key=lambda s: -min(s, nz - s))
    greeted = [at_z(s) for s in z_steps]
    greeted += [at_y(k)[1] for k in range(1, ny)] + [at_xc(k)[1] for k in range(1, nxc)]
    barrier = pltpu.get_barrier_semaphore()
    for dev in greeted:
        pl.semaphore_signal(barrier, inc=1, device_id=dev, device_id_type=MESH)

    loads = [
        pltpu.make_async_copy(ref, raw.at[at], load_sem.at[at])
        for at, ref in enumerate((images, texts))
    ]
    for load in loads:
        load.start()
    temp = jnp.exp(jnp.full((1, 1), log_temp[0], F32))
    offset = bias[0]
    for at, slot in ((0, img_own), (1, txt_own)):
        loads[at].wait()
        v = raw[at]
        n = jnp.sqrt(jnp.sum(v * v, axis=-1, keepdims=True) + 1e-06)
        u = v / n
        norm[at] = n
        unit[at] = u
        slot[...] = u.astype(BF16)
    pl.semaphore_wait(barrier, len(greeted))

    pending = []

    def send(src, dst, s_sem, r_sem, dev):
        copy = remote(src, dst, s_sem, r_sem, dev)
        copy.start()
        pending.append(copy)

    def arrived(slot, sem):
        remote(slot, slot, sem, sem, at_z(1)).wait_recv()

    for i, step in enumerate(img_steps):
        send(img_own, img_way.at[i], s_iw.at[i], r_iw.at[i], at_z(step))
    for i, step in enumerate(txt_steps):
        send(txt_own, txt_way.at[i], s_tw.at[i], r_tw.at[i], at_z(step))
    for i in range(len(img_steps)):
        arrived(img_way.at[i], r_iw.at[i])
    for i in range(len(txt_steps)):
        arrived(txt_way.at[i], r_tw.at[i])
    hops = [(way, step) for way, after in enumerate(img_next) for step in after]
    for i, (way, step) in enumerate(hops):
        send(img_way.at[way], img_all.at[xc, i], s_iz.at[i], r_iz.at[i], at_z(step))
    for i, step in reversed(list(enumerate(txt_next))):
        send(txt_way, txt_all.at[y, i], s_tz.at[i], r_tz.at[i], at_z(step))
    half = max(1, len(txt_next) // 2)
    batches = [pl.ds(i, half) for i in range(0, len(txt_next), half)]

    def text_batch(n):
        for i in range(n * half, n * half + half):
            arrived(txt_all.at[y, i], r_tz.at[i])
        for k in range(1, ny):
            to, dev = at_y(k)
            block = txt_all.at[y, batches[n]]
            send(block, block, s_ty.at[n, to], r_ty.at[n, y], dev)

    pairs_of = [pl.ds(0, 2), pl.ds(2, 2)]

    def image_batch(n):
        for i in (2 * n, 2 * n + 1):
            arrived(img_all.at[xc, i], r_iz.at[i])
        for k in range(1, nxc):
            to, dev = at_xc(k)
            block = img_all.at[xc, pairs_of[n]]
            send(block, block, s_ix.at[n, to], r_ix.at[n, xc], dev)

    text_batch(0)
    image_batch(1)
    for n in range(1, len(batches)):
        text_batch(n)
    image_batch(0)
    for n, batch in enumerate(batches):
        for k in range(1, ny):
            to, _ = at_y(k)
            arrived(txt_all.at[to, batch], r_ty.at[n, to])
    for n in (1, 0):
        for k in range(1, nxc):
            to, _ = at_xc(k)
            arrived(img_all.at[to, pairs_of[n]], r_ix.at[n, to])

    n_img, n_txt = nxc * na * own, ny * nb * own
    img = img_all[...].astype(F32).reshape(n_img, width).astype(BF16)
    txt = txt_all[...].astype(F32).reshape(n_txt, width).astype(BF16)
    scores = lax.dot_general(txt, img, (((1,), (1,)), ((), ())), preferred_element_type=F32)
    at_i = lax.broadcasted_iota(jnp.int32, (1, n_img), 1)
    at_t = lax.broadcasted_iota(jnp.int32, (n_txt, 1), 0)

    def stepped(steps, index):
        value = jnp.zeros_like(index)
        for i, s in enumerate(steps):
            value = jnp.where(index == i, s, value)
        return value

    i_xc, i_z = at_i // (na * own), (z + nz - stepped(img_to, (at_i // own) % na)) % nz
    t_y, t_z = at_t // (nb * own), (z + nz - stepped(txt_to, (at_t // own) % nb)) % nz
    i_row, i_col = device(i_xc // nc, y, i_xc % nc, i_z)
    t_row, t_col = device(x, t_y, core, t_z)
    rows, cols = nx * nzh * nc, ny * nzl
    i_id = (i_row * cols + i_col) * own + at_i % own
    t_id = (t_col * rows + t_row) * own + at_t % own
    same = i_id == t_id
    logits = temp * scores + offset
    margin = jnp.where(same, -logits, logits)
    e = jnp.exp(-jnp.abs(margin))
    sig = jnp.where(margin >= 0, 1.0, e) / (1.0 + e)
    dlogit = jnp.where(same, -sig, sig)
    loss = jnp.maximum(margin, 0.0) + jnp.log1p(e)

    def total(v):
        return jnp.sum(jnp.sum(v, axis=0, keepdims=True), axis=1, keepdims=True)

    lane = lax.broadcasted_iota(jnp.int32, (1, 128), 1)
    sc_near[q] = jnp.where(
        lane == 0, total(loss), jnp.where(lane == 1, total(dlogit * scores), total(dlogit))
    )
    for k in range(1, nq):
        to = lax.rem(q + k, nq)
        dev = device(to // (ny * nc), (to // nc) % ny, lax.rem(to, nc), z)
        remote(sc_near.at[q], sc_near.at[q], s_sn, r_sn, dev).start()
    low = dlogit.astype(BF16)
    img_part = lax.dot_general(low, txt, (((0,), (0,)), ((), ())), preferred_element_type=F32)
    img_out[...] = img_part.reshape(nxc, na, own, width).astype(BF16)
    for n, pair in enumerate(pairs_of):
        for k in range(1, nxc):
            to, dev = at_xc(k)
            send(img_out.at[to, pair], img_in.at[xc, pair], s_bx.at[n, to], r_bx.at[n, xc], dev)
    txt_part = jnp.dot(low, img, preferred_element_type=F32)
    txt_out[...] = txt_part.reshape(ny, nb // 2, 2, own, width).astype(BF16)
    for n, batch in reversed(list(enumerate(batches))):
        for k in range(1, ny):
            to, dev = at_y(k)
            send(txt_out.at[to, batch], txt_in.at[y, batch], s_by.at[n, to], r_by.at[n, y], dev)

    remote(sc_near.at[pl.ds(0, nq - 1)], sc_near.at[pl.ds(0, nq - 1)], s_sn, r_sn, at_z(1)).wait_recv()
    sc_z[z] = jnp.sum(sc_near[...], axis=0)
    offsets = sorted((s for s in range(-nz // 2 + 1, nz // 2 + 1)), key=lambda s: -abs(s))
    straight = [s for s in offsets if s != 0 and -reach[0] <= s <= reach[1]]
    relayed = [s for s in offsets if s not in straight and s != 0]
    legs = [(s - relay, relay) if s > 0 else (s + relay, -relay) for s in relayed]
    first = [leg for leg, _ in legs]
    for s in straight:
        sem = r_relay.at[first.index(s)] if s in first else r_sz
        remote(sc_z.at[z], sc_z.at[z], s_sz, sem, at_z(s)).start()

    for n, pair in enumerate(pairs_of):
        acc = img_out[xc, pair].astype(F32)
        for k in range(1, nxc):
            to, _ = at_xc(k)
            arrived(img_in.at[to, pair], r_bx.at[n, to])
            acc += img_in[to, pair].astype(F32)
        img_zout[pair] = acc.astype(BF16)
        for i in (2 * n, 2 * n + 1):
            send(img_zout.at[i], img_zin.at[i], s_bi.at[i], r_bi.at[i], at_z(-img_to[i]))
    for n, batch in reversed(list(enumerate(batches))):
        acc = txt_out[y, batch].astype(F32)
        for k in range(1, ny):
            to, _ = at_y(k)
            arrived(txt_in.at[to, batch], r_by.at[n, to])
            acc += txt_in[to, batch].astype(F32)
        txt_zout[batch] = acc.astype(BF16)
        for i in range(n * half, n * half + half):
            for j in range(2):
                at = i * 2 + j
                send(txt_zout.at[i, j], txt_zin.at[at], s_bt.at[at], r_bt.at[at], at_z(-txt_to[at]))

    for n, (leg, on) in enumerate(legs):
        slot = sc_z.at[lax.rem(z - leg + nz, nz)]
        arrived(slot, r_relay.at[n])
        remote(slot, slot, s_sz, r_sz, at_z(on)).start()

    def finish(at, gathered, sem, out):
        for i in range(gathered.shape[0]):
            arrived(gathered.at[i], sem.at[i])
        g = temp * jnp.sum(gathered[...].astype(F32), axis=0)
        u = unit[at]
        along = jnp.sum(u * g, axis=-1, keepdims=True)
        out[...] = (g - u * along) / norm[at]

    finish(1, txt_zin, r_bt, text_grad)
    finish(0, img_zin, r_bi, image_grad)

    for copy in pending:
        copy.wait_send()
    rest = sc_near.at[pl.ds(0, nq - 1)]
    remote(rest, rest, s_sn, r_sn, at_z(1)).wait_send()
    rest = sc_z.at[pl.ds(0, nz - 1)]
    remote(rest, rest, s_sz, r_sz, at_z(1)).wait_send()
    rest = sc_z.at[pl.ds(0, nz - 1 - len(legs))]
    remote(rest, rest, s_sz, r_sz, at_z(1)).wait_recv()
    pairs = float(rows * cols * own)
    scale = 1.0 / (pairs * pairs)
    result = jnp.sum(sc_z[...], axis=0) * scale
    terms[...] = jnp.where(lane == 1, temp, 1.0) * result


def on_device(factors, images, texts, log_temp, bias):
    nx, nzh, nc, ny, nzl = (factors[k] for k in ("nx", "nzh", "nc", "ny", "nzl"))
    nxc, na, nn = nx * nc, sum(len(n) for n in factors["img_next"]), len(factors["txt_next"])
    nb, nw = 2 * nn, max(1, nn // (nn // 2 or 1))
    own, width = images.shape
    vmem = pl.BlockSpec(memory_space=pltpu.VMEM)
    smem = pl.BlockSpec(memory_space=pltpu.SMEM)
    hbm = pl.BlockSpec(memory_space=pl.ANY)

    def low(*lead):
        return pltpu.VMEM(lead + (own, width), BF16)

    def sems(*counts):
        return [pltpu.SemaphoreType.DMA(c) for c in counts for _ in range(2)]

    image_grad, text_grad, terms = pl.pallas_call(
        functools.partial(kernel, *factors.values()),
        out_shape=(
            jax.ShapeDtypeStruct((own, width), F32),
            jax.ShapeDtypeStruct((own, width), F32),
            jax.ShapeDtypeStruct((1, 128), F32),
        ),
        in_specs=[hbm, hbm, smem, smem],
        out_specs=(vmem, vmem, vmem),
        scratch_shapes=[
            pltpu.VMEM((2, own, width), F32),
            pltpu.VMEM((2, own, width), F32),
            pltpu.VMEM((2, own, 1), F32),
            low(), low(), low(2), low(2),
            low(nxc, na), low(ny, nn, 2),
            low(nxc, na), low(ny, nn, 2), low(nxc, na), low(ny, nn, 2),
            low(na), low(nn, 2), low(na), low(nb),
            pltpu.VMEM((nx * ny * nc, 1, 128), F32),
            pltpu.VMEM((nzh * nzl, 1, 128), F32),
            pltpu.SemaphoreType.DMA((2,)),
        ] + sems(
            (2,), (2,), (na,), (nn,), (2, nxc), (nw, ny), (2, nxc), (nw, ny), (na,), (nb,), (), ()
        ) + [pltpu.SemaphoreType.DMA((8,))],
        compiler_params=pltpu.CompilerParams(
            collective_id=0, has_side_effects=True
        ),
    )(images, texts, log_temp, bias)
    return image_grad, text_grad, terms[0, 0], terms[0, 1], terms[0, 2]


def solution(mesh, factors=FACTORS):
    in_specs = (P(("row", "col"), None), P(("col", "row"), None), P(), P())
    out_specs = (P(("row", "col"), None), P(("col", "row"), None), P(), P(), P())
    return jax.shard_map(
        functools.partial(on_device, factors),
        mesh=mesh, in_specs=in_specs, out_specs=out_specs, check_vma=False,
    )
```

```python
import functools

import jax
import jax.numpy as jnp
from jax import lax
from jax.experimental import pallas as pl
from jax.experimental.pallas import tpu as pltpu
from jax.sharding import PartitionSpec as P

MESH = pl.DeviceIdType.MESH
F32 = jnp.float32
BF16 = jnp.bfloat16

FACTORS = dict(
    nx=4, nzh=2, nc=2, ny=4, nzl=16,
    img_steps=(4, -4), img_next=((5, 4), (-4, -3)), txt_steps=(4, -4), txt_next=(1, -1, 3, -3),
    greet=(4, 3, 2, 1), far=8,
)


def remote(src, dst, send, recv, dev):
    return pltpu.make_async_remote_copy(
        src_ref=src, dst_ref=dst, send_sem=send, recv_sem=recv, device_id=dev, device_id_type=MESH
    )


def kernel(
    nx, nzh, nc, ny, nzl, img_steps, img_next, txt_steps, txt_next, greet, far,
    images, texts, log_temp, bias,
    image_grad, text_grad, terms,
    raw, unit, norm, img_own, txt_own, img_way, txt_way, img_all, txt_all, img_out, txt_out, img_in, txt_in,
    img_zout, txt_zout, img_zin, txt_zin, sc_near, sc_z, load_sem,
    s_iw, r_iw, s_tw, r_tw, s_iz, r_iz, s_tz, r_tz, s_ix, r_ix, s_ty, r_ty,
    s_bx, r_bx, s_by, r_by, s_bi, r_bi, s_bt, r_bt, s_sn, r_sn, s_sz, r_sz, ready,
):
    own, width = images.shape
    nz, nxc, nq = nzh * nzl, nx * nc, nx * ny * nc
    img_to = [a + b for a, after in zip(img_steps, img_next) for b in after]
    txt_to = [a + b for b in txt_next for a in txt_steps]
    na, nb = len(img_to), len(txt_to)
    row, col = lax.axis_index("row"), lax.axis_index("col")
    x, zh, core = row // (nzh * nc), (row // nc) % nzh, row % nc
    y, zl = col // nzl, col % nzl
    z, xc, q = zh * nzl + zl, x * nc + core, (x * ny + y) * nc + core

    def device(x_, y_, core_, z_):
        return ((x_ * nzh + z_ // nzl) * nc + core_, y_ * nzl + z_ % nzl)

    def at_z(step):
        return device(x, y, core, lax.rem(z + (step + nz), nz))

    def at_xc(k):
        to = lax.rem(xc + k, nxc)
        return to, device(to // nc, y, lax.rem(to, nc), z)

    def at_y(k):
        to = lax.rem(y + k, ny)
        return to, device(x, to, core, z)

    z_steps = sorted({s % nz for a in greet for s in (a, -a)}, key=lambda s: -min(s, nz - s))
    greeted = [at_z(s) for s in z_steps]
    greeted += [at_y(k)[1] for k in range(1, ny)] + [at_xc(k)[1] for k in range(1, nxc)]
    barrier = pltpu.get_barrier_semaphore()
    for dev in greeted:
        pl.semaphore_signal(barrier, inc=1, device_id=dev, device_id_type=MESH)

    loads = [
        pltpu.make_async_copy(ref, raw.at[at], load_sem.at[at])
        for at, ref in enumerate((images, texts))
    ]
    for load in loads:
        load.start()
    temp = jnp.exp(jnp.full((1, 1), log_temp[0], F32))
    offset = bias[0]
    for at, slot in ((0, img_own), (1, txt_own)):
        loads[at].wait()
        v = raw[at]
        n = jnp.sqrt(jnp.sum(v * v, axis=-1, keepdims=True) + 1e-06)
        u = v / n
        norm[at] = n
        unit[at] = u
        slot[...] = u.astype(BF16)
    pl.semaphore_wait(barrier, len(greeted))

    pending = []

    def send(src, dst, s_sem, r_sem, dev):
        copy = remote(src, dst, s_sem, r_sem, dev)
        copy.start()
        pending.append(copy)

    def arrived(slot, sem):
        remote(slot, slot, sem, sem, at_z(1)).wait_recv()

    for i, step in enumerate(img_steps):
        send(img_own, img_way.at[i], s_iw.at[i], r_iw.at[i], at_z(step))
    for i, step in enumerate(txt_steps):
        send(txt_own, txt_way.at[i], s_tw.at[i], r_tw.at[i], at_z(step))
    for i in range(len(img_steps)):
        arrived(img_way.at[i], r_iw.at[i])
    for i in range(len(txt_steps)):
        arrived(txt_way.at[i], r_tw.at[i])
    for step in (far, -far):
        pl.semaphore_signal(ready, inc=1, device_id=at_z(step), device_id_type=MESH)
    hops = [(way, step) for way, after in enumerate(img_next) for step in after]
    for i, (way, step) in enumerate(hops):
        send(img_way.at[way], img_all.at[xc, i], s_iz.at[i], r_iz.at[i], at_z(step))
    for i, step in reversed(list(enumerate(txt_next))):
        send(txt_way, txt_all.at[y, i], s_tz.at[i], r_tz.at[i], at_z(step))
    half = max(1, len(txt_next) // 2)
    batches = [pl.ds(i, half) for i in range(0, len(txt_next), half)]

    def text_batch(n):
        for i in range(n * half, n * half + half):
            arrived(txt_all.at[y, i], r_tz.at[i])
        for k in range(1, ny):
            to, dev = at_y(k)
            block = txt_all.at[y, batches[n]]
            send(block, block, s_ty.at[n, to], r_ty.at[n, y], dev)

    pairs_of = [pl.ds(0, 2), pl.ds(2, 2)]

    def image_batch(n):
        for i in (2 * n, 2 * n + 1):
            arrived(img_all.at[xc, i], r_iz.at[i])
        for k in range(1, nxc):
            to, dev = at_xc(k)
            block = img_all.at[xc, pairs_of[n]]
            send(block, block, s_ix.at[n, to], r_ix.at[n, xc], dev)

    text_batch(0)
    image_batch(1)
    for n in range(1, len(batches)):
        text_batch(n)
    image_batch(0)
    for n, batch in enumerate(batches):
        for k in range(1, ny):
            to, _ = at_y(k)
            arrived(txt_all.at[to, batch], r_ty.at[n, to])
    for n in (1, 0):
        for k in range(1, nxc):
            to, _ = at_xc(k)
            arrived(img_all.at[to, pairs_of[n]], r_ix.at[n, to])

    n_img, n_txt = nxc * na * own, ny * nb * own
    img = img_all[...].astype(F32).reshape(n_img, width).astype(BF16)
    txt = txt_all[...].astype(F32).reshape(n_txt, width).astype(BF16)
    scores = lax.dot_general(txt, img, (((1,), (1,)), ((), ())), preferred_element_type=F32)
    at_i = lax.broadcasted_iota(jnp.int32, (1, n_img), 1)
    at_t = lax.broadcasted_iota(jnp.int32, (n_txt, 1), 0)

    def stepped(steps, index):
        value = jnp.zeros_like(index)
        for i, s in enumerate(steps):
            value = jnp.where(index == i, s, value)
        return value

    i_xc, i_z = at_i // (na * own), (z + nz - stepped(img_to, (at_i // own) % na)) % nz
    t_y, t_z = at_t // (nb * own), (z + nz - stepped(txt_to, (at_t // own) % nb)) % nz
    i_row, i_col = device(i_xc // nc, y, i_xc % nc, i_z)
    t_row, t_col = device(x, t_y, core, t_z)
    rows, cols = nx * nzh * nc, ny * nzl
    i_id = (i_row * cols + i_col) * own + at_i % own
    t_id = (t_col * rows + t_row) * own + at_t % own
    same = i_id == t_id
    logits = temp * scores + offset
    margin = jnp.where(same, -logits, logits)
    e = jnp.exp(-jnp.abs(margin))
    sig = jnp.where(margin >= 0, 1.0, e) / (1.0 + e)
    dlogit = jnp.where(same, -sig, sig)
    loss = jnp.maximum(margin, 0.0) + jnp.log1p(e)

    def total(v):
        return jnp.sum(jnp.sum(v, axis=0, keepdims=True), axis=1, keepdims=True)

    lane = lax.broadcasted_iota(jnp.int32, (1, 128), 1)
    sc_z[z] = jnp.where(
        lane == 0, total(loss), jnp.where(lane == 1, total(dlogit * scores), total(dlogit))
    )
    pl.semaphore_wait(ready, 2)
    for step in sorted(range(1, nz), key=lambda s: -min(s, nz - s)):
        remote(sc_z.at[z], sc_z.at[z], s_sz, r_sz, at_z(step)).start()
    low = dlogit.astype(BF16)
    img_part = lax.dot_general(low, txt, (((0,), (0,)), ((), ())), preferred_element_type=F32)
    img_out[...] = img_part.reshape(nxc, na, own, width).astype(BF16)
    for n, pair in enumerate(pairs_of):
        for k in range(1, nxc):
            to, dev = at_xc(k)
            send(img_out.at[to, pair], img_in.at[xc, pair], s_bx.at[n, to], r_bx.at[n, xc], dev)
    txt_part = jnp.dot(low, img, preferred_element_type=F32)
    txt_out[...] = txt_part.reshape(ny, nb // 2, 2, own, width).astype(BF16)
    for n, batch in reversed(list(enumerate(batches))):
        for k in range(1, ny):
            to, dev = at_y(k)
            send(txt_out.at[to, batch], txt_in.at[y, batch], s_by.at[n, to], r_by.at[n, y], dev)

    for n, pair in enumerate(pairs_of):
        acc = img_out[xc, pair].astype(F32)
        for k in range(1, nxc):
            to, _ = at_xc(k)
            arrived(img_in.at[to, pair], r_bx.at[n, to])
            acc += img_in[to, pair].astype(F32)
        img_zout[pair] = acc.astype(BF16)
        for i in (2 * n, 2 * n + 1):
            send(img_zout.at[i], img_zin.at[i], s_bi.at[i], r_bi.at[i], at_z(-img_to[i]))
    for n, batch in reversed(list(enumerate(batches))):
        acc = txt_out[y, batch].astype(F32)
        for k in range(1, ny):
            to, _ = at_y(k)
            arrived(txt_in.at[to, batch], r_by.at[n, to])
            acc += txt_in[to, batch].astype(F32)
        txt_zout[batch] = acc.astype(BF16)
        for i in range(n * half, n * half + half):
            for j in range(2):
                at = i * 2 + j
                send(txt_zout.at[i, j], txt_zin.at[at], s_bt.at[at], r_bt.at[at], at_z(-txt_to[at]))

    others = sc_z.at[pl.ds(0, nz - 1)]
    remote(others, others, s_sz, r_sz, at_z(1)).wait_recv()
    sc_near[q] = jnp.sum(sc_z[...], axis=0)
    for k in range(1, nq):
        to = lax.rem(q + k, nq)
        dev = device(to // (ny * nc), (to // nc) % ny, lax.rem(to, nc), z)
        remote(sc_near.at[q], sc_near.at[q], s_sn, r_sn, dev).start()

    def finish(at, gathered, sem, out):
        for i in range(gathered.shape[0]):
            arrived(gathered.at[i], sem.at[i])
        g = temp * jnp.sum(gathered[...].astype(F32), axis=0)
        u = unit[at]
        along = jnp.sum(u * g, axis=-1, keepdims=True)
        out[...] = (g - u * along) / norm[at]

    finish(1, txt_zin, r_bt, text_grad)
    finish(0, img_zin, r_bi, image_grad)

    for copy in pending:
        copy.wait_send()
    remote(others, others, s_sz, r_sz, at_z(1)).wait_send()
    rest = sc_near.at[pl.ds(0, nq - 1)]
    remote(rest, rest, s_sn, r_sn, at_z(1)).wait_send()
    remote(rest, rest, s_sn, r_sn, at_z(1)).wait_recv()
    pairs = float(rows * cols * own)
    scale = 1.0 / (pairs * pairs)
    result = jnp.sum(sc_near[...], axis=0) * scale
    terms[...] = jnp.where(lane == 1, temp, 1.0) * result


def on_device(factors, images, texts, log_temp, bias):
    nx, nzh, nc, ny, nzl = (factors[k] for k in ("nx", "nzh", "nc", "ny", "nzl"))
    nxc, na, nn = nx * nc, sum(len(n) for n in factors["img_next"]), len(factors["txt_next"])
    nb, nw = 2 * nn, max(1, nn // (nn // 2 or 1))
    own, width = images.shape
    vmem = pl.BlockSpec(memory_space=pltpu.VMEM)
    smem = pl.BlockSpec(memory_space=pltpu.SMEM)
    hbm = pl.BlockSpec(memory_space=pl.ANY)

    def low(*lead):
        return pltpu.VMEM(lead + (own, width), BF16)

    def sems(*counts):
        return [pltpu.SemaphoreType.DMA(c) for c in counts for _ in range(2)]

    image_grad, text_grad, terms = pl.pallas_call(
        functools.partial(kernel, *factors.values()),
        out_shape=(
            jax.ShapeDtypeStruct((own, width), F32),
            jax.ShapeDtypeStruct((own, width), F32),
            jax.ShapeDtypeStruct((1, 128), F32),
        ),
        in_specs=[hbm, hbm, smem, smem],
        out_specs=(vmem, vmem, vmem),
        scratch_shapes=[
            pltpu.VMEM((2, own, width), F32),
            pltpu.VMEM((2, own, width), F32),
            pltpu.VMEM((2, own, 1), F32),
            low(), low(), low(2), low(2),
            low(nxc, na), low(ny, nn, 2),
            low(nxc, na), low(ny, nn, 2), low(nxc, na), low(ny, nn, 2),
            low(na), low(nn, 2), low(na), low(nb),
            pltpu.VMEM((nx * ny * nc, 1, 128), F32),
            pltpu.VMEM((nzh * nzl, 1, 128), F32),
            pltpu.SemaphoreType.DMA((2,)),
        ] + sems(
            (2,), (2,), (na,), (nn,), (2, nxc), (nw, ny), (2, nxc), (nw, ny), (na,), (nb,), (), ()
        ) + [pltpu.SemaphoreType.REGULAR],
        compiler_params=pltpu.CompilerParams(
            collective_id=0, has_side_effects=True
        ),
    )(images, texts, log_temp, bias)
    return image_grad, text_grad, terms[0, 0], terms[0, 1], terms[0, 2]


def solution(mesh, factors=FACTORS):
    in_specs = (P(("row", "col"), None), P(("col", "row"), None), P(), P())
    out_specs = (P(("row", "col"), None), P(("col", "row"), None), P(), P(), P())
    return jax.shard_map(
        functools.partial(on_device, factors),
        mesh=mesh, in_specs=in_specs, out_specs=out_specs, check_vma=False,
    )
```

```python
import functools

import jax
import jax.numpy as jnp
from jax import lax
from jax.experimental import pallas as pl
from jax.experimental.pallas import tpu as pltpu
from jax.sharding import PartitionSpec as P

MESH = pl.DeviceIdType.MESH
F32 = jnp.float32
BF16 = jnp.bfloat16

FACTORS = dict(
    nx=4, nzh=2, nc=2, ny=4, nzl=16,
    img_steps=(4, -4), img_next=((5, 4), (-4, -3)), txt_steps=(4, -4), txt_next=(1, -1, 3, -3),
    greet=(4, 3, 2, 1), far=8,
)


def remote(src, dst, send, recv, dev):
    return pltpu.make_async_remote_copy(
        src_ref=src, dst_ref=dst, send_sem=send, recv_sem=recv, device_id=dev, device_id_type=MESH
    )


def kernel(
    nx, nzh, nc, ny, nzl, img_steps, img_next, txt_steps, txt_next, greet, far,
    images, texts, log_temp, bias,
    grads, terms,
    raw, unit, norm, img_own, txt_own, img_way, txt_way, img_all, txt_all, img_out, txt_out, img_in, txt_in,
    img_zout, txt_zout, img_zin, txt_zin, sc_near, sc_z, held, load_sem,
    s_iw, r_iw, s_tw, r_tw, s_iz, r_iz, s_tz, r_tz, s_ix, r_ix, s_ty, r_ty,
    s_bx, r_bx, s_by, r_by, s_bi, r_bi, s_bt, r_bt, s_sn, r_sn, s_sz, r_sz, ready,
):
    own, width = images.shape
    nz, nxc, nq = nzh * nzl, nx * nc, nx * ny * nc
    img_to = [a + b for a, after in zip(img_steps, img_next) for b in after]
    txt_to = [a + b for b in txt_next for a in txt_steps]
    na, nb = len(img_to), len(txt_to)
    row, col = lax.axis_index("row"), lax.axis_index("col")
    x, zh, core = row // (nzh * nc), (row // nc) % nzh, row % nc
    y, zl = col // nzl, col % nzl
    z, xc, q = zh * nzl + zl, x * nc + core, (x * ny + y) * nc + core

    def device(x_, y_, core_, z_):
        return ((x_ * nzh + z_ // nzl) * nc + core_, y_ * nzl + z_ % nzl)

    def at_z(step):
        return device(x, y, core, lax.rem(z + (step + nz), nz))

    def at_xc(k):
        to = lax.rem(xc + k, nxc)
        return to, device(to // nc, y, lax.rem(to, nc), z)

    def at_y(k):
        to = lax.rem(y + k, ny)
        return to, device(x, to, core, z)

    z_steps = sorted({s % nz for a in greet for s in (a, -a)}, key=lambda s: -min(s, nz - s))
    greeted = [at_z(s) for s in z_steps]
    greeted += [at_y(k)[1] for k in range(1, ny)] + [at_xc(k)[1] for k in range(1, nxc)]
    barrier = pltpu.get_barrier_semaphore()
    for dev in greeted:
        pl.semaphore_signal(barrier, inc=1, device_id=dev, device_id_type=MESH)

    loads = [
        pltpu.make_async_copy(ref, to, load_sem.at[at])
        for at, (ref, to) in enumerate(
            ((images, raw.at[0]), (texts, raw.at[1]), (log_temp, held.at[0]), (bias, held.at[1]))
        )
    ]
    for load in loads:
        load.start()
    for at, slot in ((0, img_own), (1, txt_own)):
        loads[at].wait()
        v = raw[at]
        n = jnp.sqrt(jnp.sum(v * v, axis=-1, keepdims=True) + 1e-06)
        u = v / n
        norm[at] = n
        unit[at] = u
        slot[...] = u.astype(BF16)
    for load in loads[2:]:
        load.wait()
    temp = jnp.exp(jnp.full((1, 1), held[0, 0], F32))
    offset = held[1, 0]
    pl.semaphore_wait(barrier, len(greeted))

    pending = []

    def send(src, dst, s_sem, r_sem, dev):
        copy = remote(src, dst, s_sem, r_sem, dev)
        copy.start()
        pending.append(copy)

    def arrived(slot, sem):
        remote(slot, slot, sem, sem, at_z(1)).wait_recv()

    for i, step in enumerate(img_steps):
        send(img_own, img_way.at[i], s_iw.at[i], r_iw.at[i], at_z(step))
    for i, step in enumerate(txt_steps):
        send(txt_own, txt_way.at[i], s_tw.at[i], r_tw.at[i], at_z(step))
    for i in range(len(img_steps)):
        arrived(img_way.at[i], r_iw.at[i])
    for i in range(len(txt_steps)):
        arrived(txt_way.at[i], r_tw.at[i])
    for step in (far, -far):
        pl.semaphore_signal(ready, inc=1, device_id=at_z(step), device_id_type=MESH)
    hops = [(way, step) for way, after in enumerate(img_next) for step in after]
    for i, (way, step) in enumerate(hops):
        send(img_way.at[way], img_all.at[xc, i], s_iz.at[i], r_iz.at[i], at_z(step))
    for i, step in reversed(list(enumerate(txt_next))):
        send(txt_way, txt_all.at[y, i], s_tz.at[i], r_tz.at[i], at_z(step))
    half = max(1, len(txt_next) // 2)
    batches = [pl.ds(i, half) for i in range(0, len(txt_next), half)]

    def text_batch(n):
        for i in range(n * half, n * half + half):
            arrived(txt_all.at[y, i], r_tz.at[i])
        for k in range(1, ny):
            to, dev = at_y(k)
            block = txt_all.at[y, batches[n]]
            send(block, block, s_ty.at[n, to], r_ty.at[n, y], dev)

    pairs_of = [pl.ds(0, 2), pl.ds(2, 2)]

    def image_batch(n):
        for i in (2 * n, 2 * n + 1):
            arrived(img_all.at[xc, i], r_iz.at[i])
        for k in range(1, nxc):
            to, dev = at_xc(k)
            block = img_all.at[xc, pairs_of[n]]
            send(block, block, s_ix.at[n, to], r_ix.at[n, xc], dev)

    text_batch(0)
    image_batch(1)
    for n in range(1, len(batches)):
        text_batch(n)
    image_batch(0)
    for n, batch in enumerate(batches):
        for k in range(1, ny):
            to, _ = at_y(k)
            arrived(txt_all.at[to, batch], r_ty.at[n, to])
    for n in (1, 0):
        for k in range(1, nxc):
            to, _ = at_xc(k)
            arrived(img_all.at[to, pairs_of[n]], r_ix.at[n, to])

    n_img, n_txt = nxc * na * own, ny * nb * own
    img = img_all[...].astype(F32).reshape(n_img, width).astype(BF16)
    txt = txt_all[...].astype(F32).reshape(n_txt, width).astype(BF16)
    scores = lax.dot_general(txt, img, (((1,), (1,)), ((), ())), preferred_element_type=F32)
    at_i = lax.broadcasted_iota(jnp.int32, (1, n_img), 1)
    at_t = lax.broadcasted_iota(jnp.int32, (n_txt, 1), 0)

    def stepped(steps, index):
        value = jnp.zeros_like(index)
        for i, s in enumerate(steps):
            value = jnp.where(index == i, s, value)
        return value

    i_xc, i_z = at_i // (na * own), (z + nz - stepped(img_to, (at_i // own) % na)) % nz
    t_y, t_z = at_t // (nb * own), (z + nz - stepped(txt_to, (at_t // own) % nb)) % nz
    i_row, i_col = device(i_xc // nc, y, i_xc % nc, i_z)
    t_row, t_col = device(x, t_y, core, t_z)
    rows, cols = nx * nzh * nc, ny * nzl
    i_id = (i_row * cols + i_col) * own + at_i % own
    t_id = (t_col * rows + t_row) * own + at_t % own
    same = i_id == t_id
    logits = temp * scores + offset
    margin = jnp.where(same, -logits, logits)
    e = jnp.exp(-jnp.abs(margin))
    sig = jnp.where(margin >= 0, 1.0, e) / (1.0 + e)
    dlogit = jnp.where(same, -sig, sig)
    loss = jnp.maximum(margin, 0.0) + jnp.log1p(e)

    def total(v):
        return jnp.sum(jnp.sum(v, axis=0, keepdims=True), axis=1, keepdims=True)

    lane = lax.broadcasted_iota(jnp.int32, (1, 128), 1)
    sc_z[z] = jnp.where(
        lane == 0, total(loss), jnp.where(lane == 1, total(dlogit * scores), total(dlogit))
    )
    pl.semaphore_wait(ready, 2)
    for step in sorted(range(1, nz), key=lambda s: -min(s, nz - s)):
        remote(sc_z.at[z], sc_z.at[z], s_sz, r_sz, at_z(step)).start()
    low = dlogit.astype(BF16)
    img_part = lax.dot_general(low, txt, (((0,), (0,)), ((), ())), preferred_element_type=F32)
    img_out[...] = img_part.reshape(nxc, na, own, width).astype(BF16)
    for n, pair in enumerate(pairs_of):
        for k in range(1, nxc):
            to, dev = at_xc(k)
            send(img_out.at[to, pair], img_in.at[xc, pair], s_bx.at[n, to], r_bx.at[n, xc], dev)
    txt_part = jnp.dot(low, img, preferred_element_type=F32)
    txt_out[...] = txt_part.reshape(ny, nb // 2, 2, own, width).astype(BF16)
    for n, batch in reversed(list(enumerate(batches))):
        for k in range(1, ny):
            to, dev = at_y(k)
            send(txt_out.at[to, batch], txt_in.at[y, batch], s_by.at[n, to], r_by.at[n, y], dev)

    def return_images(n):
        pair = pairs_of[n]
        acc = img_out[xc, pair].astype(F32)
        for k in range(1, nxc):
            to, _ = at_xc(k)
            arrived(img_in.at[to, pair], r_bx.at[n, to])
            acc += img_in[to, pair].astype(F32)
        img_zout[pair] = acc.astype(BF16)
        for i in (2 * n, 2 * n + 1):
            send(img_zout.at[i], img_zin.at[i], s_bi.at[i], r_bi.at[i], at_z(-img_to[i]))

    def return_texts(n):
        batch = batches[n]
        acc = txt_out[y, batch].astype(F32)
        for k in range(1, ny):
            to, _ = at_y(k)
            arrived(txt_in.at[to, batch], r_by.at[n, to])
            acc += txt_in[to, batch].astype(F32)
        txt_zout[batch] = acc.astype(BF16)
        for i in range(n * half, n * half + half):
            for j in range(2):
                at = i * 2 + j
                send(txt_zout.at[i, j], txt_zin.at[at], s_bt.at[at], r_bt.at[at], at_z(-txt_to[at]))

    return_images(0)
    return_texts(len(batches) - 1)
    return_images(1)
    for n in range(len(batches) - 1):
        return_texts(n)

    others = sc_z.at[pl.ds(0, nz - 1)]
    remote(others, others, s_sz, r_sz, at_z(1)).wait_recv()
    sc_near[q] = jnp.sum(sc_z[...], axis=0)
    for k in range(1, nq):
        to = lax.rem(q + k, nq)
        dev = device(to // (ny * nc), (to // nc) % ny, lax.rem(to, nc), z)
        remote(sc_near.at[q], sc_near.at[q], s_sn, r_sn, dev).start()

    def finish(at, gathered, sem):
        for i in range(gathered.shape[0]):
            arrived(gathered.at[i], sem.at[i])
        g = temp * jnp.sum(gathered[...].astype(F32), axis=0)
        u = unit[at]
        along = jnp.sum(u * g, axis=-1, keepdims=True)
        grads[at] = (g - u * along) / norm[at]

    finish(1, txt_zin, r_bt)
    finish(0, img_zin, r_bi)

    for copy in pending:
        copy.wait_send()
    remote(others, others, s_sz, r_sz, at_z(1)).wait_send()
    rest = sc_near.at[pl.ds(0, nq - 1)]
    remote(rest, rest, s_sn, r_sn, at_z(1)).wait_send()
    remote(rest, rest, s_sn, r_sn, at_z(1)).wait_recv()
    pairs = float(rows * cols * own)
    scale = 1.0 / (pairs * pairs)
    result = jnp.sum(sc_near[...], axis=0) * scale
    terms[...] = jnp.where(lane == 1, temp, 1.0) * result


def on_device(factors, images, texts, log_temp, bias):
    nx, nzh, nc, ny, nzl = (factors[k] for k in ("nx", "nzh", "nc", "ny", "nzl"))
    nxc, na, nn = nx * nc, sum(len(n) for n in factors["img_next"]), len(factors["txt_next"])
    nb, nw = 2 * nn, max(1, nn // (nn // 2 or 1))
    own, width = images.shape
    n_pairs = (nxc * na * own) * (ny * nb * own)
    vmem = pl.BlockSpec(memory_space=pltpu.VMEM)
    hbm = pl.BlockSpec(memory_space=pltpu.HBM)

    def low(*lead):
        return pltpu.VMEM(lead + (own, width), BF16)

    def sems(*counts):
        return [pltpu.SemaphoreType.DMA(c) for c in counts for _ in range(2)]

    grads, terms = pl.pallas_call(
        functools.partial(kernel, *factors.values()),
        out_shape=(
            jax.ShapeDtypeStruct((2, own, width), F32),
            jax.ShapeDtypeStruct((1, 128), F32),
        ),
        in_specs=[hbm] * 4,
        out_specs=(vmem, vmem),
        scratch_shapes=[
            pltpu.VMEM((2, own, width), F32),
            pltpu.VMEM((2, own, width), F32),
            pltpu.VMEM((2, own, 1), F32),
            low(), low(), low(2), low(2),
            low(nxc, na), low(ny, nn, 2),
            low(nxc, na), low(ny, nn, 2), low(nxc, na), low(ny, nn, 2),
            low(na), low(nn, 2), low(na), low(nb),
            pltpu.VMEM((nx * ny * nc, 1, 128), F32),
            pltpu.VMEM((nzh * nzl, 1, 128), F32),
            pltpu.SMEM((2, 1), F32),
            pltpu.SemaphoreType.DMA((4,)),
        ] + sems(
            (2,), (2,), (na,), (nn,), (2, nxc), (nw, ny), (2, nxc), (nw, ny), (na,), (nb,), (), ()
        ) + [pltpu.SemaphoreType.REGULAR],
        cost_estimate=pl.CostEstimate(flops=6 * n_pairs * width, bytes_accessed=4 * own * width * 4, transcendentals=2 * n_pairs),
        compiler_params=pltpu.CompilerParams(
            collective_id=0, has_side_effects=True, vmem_limit_bytes=32 * 1024 * 1024
        ),
    )(images, texts, log_temp, bias)
    return grads[0], grads[1], terms[0, 0], terms[0, 1], terms[0, 2]


def solution(mesh, factors=FACTORS):
    in_specs = (P(("row", "col"), None), P(("col", "row"), None), P(), P())
    out_specs = (P(("row", "col"), None), P(("col", "row"), None), P(), P(), P())
    return jax.shard_map(
        functools.partial(on_device, factors),
        mesh=mesh, in_specs=in_specs, out_specs=out_specs, check_vma=False,
    )
```

```python
import functools

import jax
import jax.numpy as jnp
from jax import lax
from jax.experimental import pallas as pl
from jax.experimental.pallas import tpu as pltpu
from jax.sharding import PartitionSpec as P

MESH = pl.DeviceIdType.MESH
F32 = jnp.float32
BF16 = jnp.bfloat16

FACTORS = dict(
    nx=4, nzh=2, nc=2, ny=4, nzl=16,
    img_steps=(4, -4), img_next=((5, 4), (-4, -3)), txt_steps=(4, -4), txt_next=(1, -1, 3, -3),
    greet=(4, 3, 2, 1), far=8,
)


def remote(src, dst, send, recv, dev):
    return pltpu.make_async_remote_copy(
        src_ref=src, dst_ref=dst, send_sem=send, recv_sem=recv, device_id=dev, device_id_type=MESH
    )


def kernel(
    nx, nzh, nc, ny, nzl, img_steps, img_next, txt_steps, txt_next, greet, far,
    images, texts, log_temp, bias,
    grads, terms,
    raw, unit, norm, img_own, txt_own, img_way, txt_way, img_all, txt_all, img_out, txt_out, img_in, txt_in,
    img_zout, txt_zout, img_zin, txt_zin, sc_near, sc_z, held, load_sem,
    s_iw, r_iw, s_tw, r_tw, s_iz, r_iz, s_tz, r_tz, s_ix, r_ix, s_ty, r_ty,
    s_bx, r_bx, s_by, r_by, s_bi, r_bi, s_bt, r_bt, s_sn, r_sn, s_sz, r_sz, ready,
):
    own, width = images.shape
    nz, nxc, nq = nzh * nzl, nx * nc, nx * ny * nc
    img_to = [a + b for a, after in zip(img_steps, img_next) for b in after]
    txt_to = [a + b for b in txt_next for a in txt_steps]
    na, nb = len(img_to), len(txt_to)
    row, col = lax.axis_index("row"), lax.axis_index("col")
    x, zh, core = row // (nzh * nc), (row // nc) % nzh, row % nc
    y, zl = col // nzl, col % nzl
    z, xc, q = zh * nzl + zl, x * nc + core, (x * ny + y) * nc + core

    def device(x_, y_, core_, z_):
        return ((x_ * nzh + z_ // nzl) * nc + core_, y_ * nzl + z_ % nzl)

    def at_z(step):
        return device(x, y, core, lax.rem(z + (step + nz), nz))

    def at_xc(k):
        to = lax.rem(xc + k, nxc)
        return to, device(to // nc, y, lax.rem(to, nc), z)

    def at_y(k):
        to = lax.rem(y + k, ny)
        return to, device(x, to, core, z)

    z_steps = sorted({s % nz for a in greet for s in (a, -a)}, key=lambda s: -min(s, nz - s))
    greeted = [at_z(s) for s in z_steps]
    greeted += [at_y(k)[1] for k in range(1, ny)] + [at_xc(k)[1] for k in range(1, nxc)]
    barrier = pltpu.get_barrier_semaphore()
    for dev in greeted:
        pl.semaphore_signal(barrier, inc=1, device_id=dev, device_id_type=MESH)

    loads = [
        pltpu.make_async_copy(ref, to, load_sem.at[at])
        for at, (ref, to) in enumerate(
            ((images, raw.at[0]), (texts, raw.at[1]), (log_temp, held.at[0]), (bias, held.at[1]))
        )
    ]
    for load in loads:
        load.start()
    for at, slot in ((0, img_own), (1, txt_own)):
        loads[at].wait()
        v = raw[at]
        n = jnp.sqrt(jnp.sum(v * v, axis=-1, keepdims=True) + 1e-06)
        u = v / n
        norm[at] = n
        unit[at] = u
        slot[...] = u.astype(BF16)
    for load in loads[2:]:
        load.wait()
    temp = jnp.exp(jnp.full((1, 1), held[0, 0], F32))
    offset = held[1, 0]
    pl.semaphore_wait(barrier, len(greeted))

    pending = []

    def send(src, dst, s_sem, r_sem, dev):
        copy = remote(src, dst, s_sem, r_sem, dev)
        copy.start()
        pending.append(copy)

    def arrived(slot, sem):
        remote(slot, slot, sem, sem, at_z(1)).wait_recv()

    for i, step in enumerate(img_steps):
        send(img_own, img_way.at[i], s_iw.at[i], r_iw.at[i], at_z(step))
    for i, step in enumerate(txt_steps):
        send(txt_own, txt_way.at[i], s_tw.at[i], r_tw.at[i], at_z(step))
    for i in range(len(img_steps)):
        arrived(img_way.at[i], r_iw.at[i])
    for i in range(len(txt_steps)):
        arrived(txt_way.at[i], r_tw.at[i])
    for step in (far, -far):
        pl.semaphore_signal(ready, inc=1, device_id=at_z(step), device_id_type=MESH)
    hops = [(way, step) for way, after in enumerate(img_next) for step in after]
    for i, (way, step) in enumerate(hops):
        send(img_way.at[way], img_all.at[xc, i], s_iz.at[i], r_iz.at[i], at_z(step))
    for i, step in reversed(list(enumerate(txt_next))):
        send(txt_way, txt_all.at[y, i], s_tz.at[i], r_tz.at[i], at_z(step))
    half = max(1, len(txt_next) // 2)
    batches = [pl.ds(i, half) for i in range(0, len(txt_next), half)]

    def text_batch(n):
        for i in range(n * half, n * half + half):
            arrived(txt_all.at[y, i], r_tz.at[i])
        for k in range(1, ny):
            to, dev = at_y(k)
            block = txt_all.at[y, batches[n]]
            send(block, block, s_ty.at[n, to], r_ty.at[n, y], dev)

    pairs_of = [pl.ds(0, 2), pl.ds(2, 2)]

    def image_batch(n):
        for i in (2 * n, 2 * n + 1):
            arrived(img_all.at[xc, i], r_iz.at[i])
        for k in range(1, nxc):
            to, dev = at_xc(k)
            block = img_all.at[xc, pairs_of[n]]
            send(block, block, s_ix.at[n, to], r_ix.at[n, xc], dev)

    text_batch(0)
    image_batch(1)
    for n in range(1, len(batches)):
        text_batch(n)
    image_batch(0)
    for n, batch in enumerate(batches):
        for k in range(1, ny):
            to, _ = at_y(k)
            arrived(txt_all.at[to, batch], r_ty.at[n, to])
    for n in (1, 0):
        for k in range(1, nxc):
            to, _ = at_xc(k)
            arrived(img_all.at[to, pairs_of[n]], r_ix.at[n, to])

    n_img, n_txt = nxc * na * own, ny * nb * own
    img = img_all[...].astype(F32).reshape(n_img, width).astype(BF16)
    txt = txt_all[...].astype(F32).reshape(n_txt, width).astype(BF16)
    scores = lax.dot_general(txt, img, (((1,), (1,)), ((), ())), preferred_element_type=F32)
    at_i = lax.broadcasted_iota(jnp.int32, (1, n_img), 1)
    at_t = lax.broadcasted_iota(jnp.int32, (n_txt, 1), 0)

    def stepped(steps, index):
        value = jnp.zeros_like(index)
        for i, s in enumerate(steps):
            value = jnp.where(index == i, s, value)
        return value

    i_xc, i_z = at_i // (na * own), (z + nz - stepped(img_to, (at_i // own) % na)) % nz
    t_y, t_z = at_t // (nb * own), (z + nz - stepped(txt_to, (at_t // own) % nb)) % nz
    i_row, i_col = device(i_xc // nc, y, i_xc % nc, i_z)
    t_row, t_col = device(x, t_y, core, t_z)
    rows, cols = nx * nzh * nc, ny * nzl
    i_id = (i_row * cols + i_col) * own + at_i % own
    t_id = (t_col * rows + t_row) * own + at_t % own
    same = i_id == t_id
    logits = temp * scores + offset
    margin = jnp.where(same, -logits, logits)
    e = jnp.exp(-jnp.abs(margin))
    sig = jnp.where(margin >= 0, 1.0, e) / (1.0 + e)
    dlogit = jnp.where(same, -sig, sig)
    loss = jnp.maximum(margin, 0.0) + jnp.log1p(e)

    def total(v):
        return jnp.sum(jnp.sum(v, axis=0, keepdims=True), axis=1, keepdims=True)

    lane = lax.broadcasted_iota(jnp.int32, (1, 128), 1)
    sc_z[z] = jnp.where(
        lane == 0, total(loss), jnp.where(lane == 1, total(dlogit * scores), total(dlogit))
    )
    pl.semaphore_wait(ready, 2)
    for step in sorted(range(1, nz), key=lambda s: -min(s, nz - s)):
        remote(sc_z.at[z], sc_z.at[z], s_sz, r_sz, at_z(step)).start()
    low = dlogit.astype(BF16)
    img_part = lax.dot_general(low, txt, (((0,), (0,)), ((), ())), preferred_element_type=F32)
    img_out[...] = img_part.reshape(nxc, na, own, width).astype(BF16)
    for n, pair in enumerate(pairs_of):
        for k in range(1, nxc):
            to, dev = at_xc(k)
            send(img_out.at[to, pair], img_in.at[xc, pair], s_bx.at[n, to], r_bx.at[n, xc], dev)
    txt_part = jnp.dot(low, img, preferred_element_type=F32)
    txt_out[...] = txt_part.reshape(ny, nb // 2, 2, own, width).astype(BF16)
    for n, batch in reversed(list(enumerate(batches))):
        for k in range(1, ny):
            to, dev = at_y(k)
            send(txt_out.at[to, batch], txt_in.at[y, batch], s_by.at[n, to], r_by.at[n, y], dev)

    def return_images(n):
        pair = pairs_of[n]
        acc = img_out[xc, pair].astype(F32)
        for k in range(1, nxc):
            to, _ = at_xc(k)
            arrived(img_in.at[to, pair], r_bx.at[n, to])
            acc += img_in[to, pair].astype(F32)
        img_zout[pair] = acc.astype(BF16)
        for i in (2 * n, 2 * n + 1):
            send(img_zout.at[i], img_zin.at[i], s_bi.at[i], r_bi.at[i], at_z(-img_to[i]))

    def return_texts(n):
        batch = batches[n]
        acc = txt_out[y, batch].astype(F32)
        for k in range(1, ny):
            to, _ = at_y(k)
            arrived(txt_in.at[to, batch], r_by.at[n, to])
            acc += txt_in[to, batch].astype(F32)
        txt_zout[batch] = acc.astype(BF16)
        for i in range(n * half, n * half + half):
            for j in range(2):
                at = i * 2 + j
                send(txt_zout.at[i, j], txt_zin.at[at], s_bt.at[at], r_bt.at[at], at_z(-txt_to[at]))

    return_images(0)
    return_texts(len(batches) - 1)
    return_images(1)
    for n in range(len(batches) - 1):
        return_texts(n)

    others = sc_z.at[pl.ds(0, nz - 1)]
    remote(others, others, s_sz, r_sz, at_z(1)).wait_recv()
    sc_near[q] = jnp.sum(sc_z[...], axis=0)
    for k in range(1, nq):
        to = lax.rem(q + k, nq)
        dev = device(to // (ny * nc), (to // nc) % ny, lax.rem(to, nc), z)
        remote(sc_near.at[q], sc_near.at[q], s_sn, r_sn, dev).start()

    def finish(at, gathered, sem):
        for i in range(gathered.shape[0]):
            arrived(gathered.at[i], sem.at[i])
        g = temp * jnp.sum(gathered[...].astype(F32), axis=0)
        u = unit[at]
        along = jnp.sum(u * g, axis=-1, keepdims=True)
        grads[at] = (g - u * along) / norm[at]

    finish(1, txt_zin, r_bt)
    finish(0, img_zin, r_bi)

    for copy in pending:
        copy.wait_send()
    remote(others, others, s_sz, r_sz, at_z(1)).wait_send()
    rest = sc_near.at[pl.ds(0, nq - 1)]
    remote(rest, rest, s_sn, r_sn, at_z(1)).wait_send()
    remote(rest, rest, s_sn, r_sn, at_z(1)).wait_recv()
    pairs = float(rows * cols * own)
    scale = 1.0 / (pairs * pairs)
    result = jnp.sum(sc_near[...], axis=0) * scale
    terms[...] = jnp.where(lane == 1, temp, 1.0) * result


def write_out(grads, terms, image_grad, text_grad, loss, slope, shift):
    image_grad[...] = grads[0]
    text_grad[...] = grads[1]
    for i, out in enumerate((loss, slope, shift)):
        out[...] = terms[:, i : i + 1]


def on_device(factors, images, texts, log_temp, bias):
    nx, nzh, nc, ny, nzl = (factors[k] for k in ("nx", "nzh", "nc", "ny", "nzl"))
    nxc, na, nn = nx * nc, sum(len(n) for n in factors["img_next"]), len(factors["txt_next"])
    nb, nw = 2 * nn, max(1, nn // (nn // 2 or 1))
    own, width = images.shape
    n_pairs = (nxc * na * own) * (ny * nb * own)
    vmem = pl.BlockSpec(memory_space=pltpu.VMEM)
    hbm = pl.BlockSpec(memory_space=pltpu.HBM)

    def low(*lead):
        return pltpu.VMEM(lead + (own, width), BF16)

    def sems(*counts):
        return [pltpu.SemaphoreType.DMA(c) for c in counts for _ in range(2)]

    grads, terms = pl.pallas_call(
        functools.partial(kernel, *factors.values()),
        out_shape=(
            jax.ShapeDtypeStruct((2, own, width), F32),
            jax.ShapeDtypeStruct((1, 128), F32),
        ),
        in_specs=[hbm] * 4,
        out_specs=(vmem, vmem),
        scratch_shapes=[
            pltpu.VMEM((2, own, width), F32),
            pltpu.VMEM((2, own, width), F32),
            pltpu.VMEM((2, own, 1), F32),
            low(), low(), low(2), low(2),
            low(nxc, na), low(ny, nn, 2),
            low(nxc, na), low(ny, nn, 2), low(nxc, na), low(ny, nn, 2),
            low(na), low(nn, 2), low(na), low(nb),
            pltpu.VMEM((nx * ny * nc, 1, 128), F32),
            pltpu.VMEM((nzh * nzl, 1, 128), F32),
            pltpu.SMEM((2, 1), F32),
            pltpu.SemaphoreType.DMA((4,)),
        ] + sems(
            (2,), (2,), (na,), (nn,), (2, nxc), (nw, ny), (2, nxc), (nw, ny), (na,), (nb,), (), ()
        ) + [pltpu.SemaphoreType.REGULAR],
        cost_estimate=pl.CostEstimate(flops=6 * n_pairs * width, bytes_accessed=4 * own * width * 4, transcendentals=2 * n_pairs),
        compiler_params=pltpu.CompilerParams(
            collective_id=0, has_side_effects=True, vmem_limit_bytes=32 * 1024 * 1024
        ),
    )(images, texts, log_temp, bias)
    one = jax.ShapeDtypeStruct((1, 1), F32)
    block = jax.ShapeDtypeStruct((own, width), F32)
    image_grad, text_grad, loss, slope, shift = pl.pallas_call(
        write_out,
        out_shape=(block, block, one, one, one),
        in_specs=[vmem] * 2,
        out_specs=(vmem,) * 5,
        compiler_params=pltpu.CompilerParams(vmem_limit_bytes=32 * 1024 * 1024),
    )(grads, terms)
    return image_grad, text_grad, loss[0, 0], slope[0, 0], shift[0, 0]


def solution(mesh, factors=FACTORS):
    in_specs = (P(("row", "col"), None), P(("col", "row"), None), P(), P())
    out_specs = (P(("row", "col"), None), P(("col", "row"), None), P(), P(), P())
    return jax.shard_map(
        functools.partial(on_device, factors),
        mesh=mesh, in_specs=in_specs, out_specs=out_specs, check_vma=False,
    )
```

```python
import functools

import jax
import jax.numpy as jnp
from jax import lax
from jax.experimental import pallas as pl
from jax.experimental.pallas import tpu as pltpu
from jax.sharding import PartitionSpec as P

MESH = pl.DeviceIdType.MESH
F32 = jnp.float32
BF16 = jnp.bfloat16

FACTORS = dict(
    nx=4, nzh=2, nc=2, ny=4, nzl=16,
    img_steps=(4, -4), img_next=((5, 4), (-4, -3)), txt_steps=(4, -4), txt_next=(1, -1, 3, -3),
    greet=(4, 3, 2, 1), far=8,
)


def remote(src, dst, send, recv, dev):
    return pltpu.make_async_remote_copy(
        src_ref=src, dst_ref=dst, send_sem=send, recv_sem=recv, device_id=dev, device_id_type=MESH
    )


def kernel(
    nx, nzh, nc, ny, nzl, img_steps, img_next, txt_steps, txt_next, greet, far,
    images, texts, log_temp, bias,
    grads_out, terms,
    raw, unit, norm, img_own, txt_own, img_way, txt_way, img_all, txt_all, img_out, txt_out, img_in, txt_in,
    img_zout, txt_zout, img_zin, txt_zin, sc_near, sc_z, held, grads, load_sem,
    s_iw, r_iw, s_tw, r_tw, s_iz, r_iz, s_tz, r_tz, s_ix, r_ix, s_ty, r_ty,
    s_bx, r_bx, s_by, r_by, s_bi, r_bi, s_bt, r_bt, s_sn, r_sn, s_sz, r_sz, ready,
):
    own, width = images.shape
    nz, nxc, nq = nzh * nzl, nx * nc, nx * ny * nc
    img_to = [a + b for a, after in zip(img_steps, img_next) for b in after]
    txt_to = [a + b for b in txt_next for a in txt_steps]
    na, nb = len(img_to), len(txt_to)
    row, col = lax.axis_index("row"), lax.axis_index("col")
    x, zh, core = row // (nzh * nc), (row // nc) % nzh, row % nc
    y, zl = col // nzl, col % nzl
    z, xc, q = zh * nzl + zl, x * nc + core, (x * ny + y) * nc + core

    def device(x_, y_, core_, z_):
        return ((x_ * nzh + z_ // nzl) * nc + core_, y_ * nzl + z_ % nzl)

    def at_z(step):
        return device(x, y, core, lax.rem(z + (step + nz), nz))

    def at_xc(k):
        to = lax.rem(xc + k, nxc)
        return to, device(to // nc, y, lax.rem(to, nc), z)

    def at_y(k):
        to = lax.rem(y + k, ny)
        return to, device(x, to, core, z)

    z_steps = sorted({s % nz for a in greet for s in (a, -a)}, key=lambda s: -min(s, nz - s))
    greeted = [at_z(s) for s in z_steps]
    greeted += [at_y(k)[1] for k in range(1, ny)] + [at_xc(k)[1] for k in range(1, nxc)]
    barrier = pltpu.get_barrier_semaphore()
    for dev in greeted:
        pl.semaphore_signal(barrier, inc=1, device_id=dev, device_id_type=MESH)

    loads = [
        pltpu.make_async_copy(ref, to, load_sem.at[at])
        for at, (ref, to) in enumerate(
            ((images, raw.at[0]), (texts, raw.at[1]), (log_temp, held.at[0]), (bias, held.at[1]))
        )
    ]
    for load in loads:
        load.start()
    for at, slot in ((0, img_own), (1, txt_own)):
        loads[at].wait()
        v = raw[at]
        n = jnp.sqrt(jnp.sum(v * v, axis=-1, keepdims=True) + 1e-06)
        u = v / n
        norm[at] = n
        unit[at] = u
        slot[...] = u.astype(BF16)
    for load in loads[2:]:
        load.wait()
    temp = jnp.exp(jnp.full((1, 1), held[0, 0], F32))
    offset = held[1, 0]
    pl.semaphore_wait(barrier, len(greeted))

    pending = []

    def send(src, dst, s_sem, r_sem, dev):
        copy = remote(src, dst, s_sem, r_sem, dev)
        copy.start()
        pending.append(copy)

    def arrived(slot, sem):
        remote(slot, slot, sem, sem, at_z(1)).wait_recv()

    for i, step in enumerate(img_steps):
        send(img_own, img_way.at[i], s_iw.at[i], r_iw.at[i], at_z(step))
    for i, step in enumerate(txt_steps):
        send(txt_own, txt_way.at[i], s_tw.at[i], r_tw.at[i], at_z(step))
    for i in range(len(img_steps)):
        arrived(img_way.at[i], r_iw.at[i])
    for i in range(len(txt_steps)):
        arrived(txt_way.at[i], r_tw.at[i])
    for step in (far, -far):
        pl.semaphore_signal(ready, inc=1, device_id=at_z(step), device_id_type=MESH)
    hops = [(way, step) for way, after in enumerate(img_next) for step in after]
    for i, (way, step) in enumerate(hops):
        send(img_way.at[way], img_all.at[xc, i], s_iz.at[i], r_iz.at[i], at_z(step))
    for i, step in reversed(list(enumerate(txt_next))):
        send(txt_way, txt_all.at[y, i], s_tz.at[i], r_tz.at[i], at_z(step))
    half = max(1, len(txt_next) // 2)
    batches = [pl.ds(i, half) for i in range(0, len(txt_next), half)]

    def text_batch(n):
        for i in range(n * half, n * half + half):
            arrived(txt_all.at[y, i], r_tz.at[i])
        for k in range(1, ny):
            to, dev = at_y(k)
            block = txt_all.at[y, batches[n]]
            send(block, block, s_ty.at[n, to], r_ty.at[n, y], dev)

    pairs_of = [pl.ds(0, 2), pl.ds(2, 2)]

    def image_batch(n):
        for i in (2 * n, 2 * n + 1):
            arrived(img_all.at[xc, i], r_iz.at[i])
        for k in range(1, nxc):
            to, dev = at_xc(k)
            block = img_all.at[xc, pairs_of[n]]
            send(block, block, s_ix.at[n, to], r_ix.at[n, xc], dev)

    text_batch(0)
    image_batch(1)
    for n in range(1, len(batches)):
        text_batch(n)
    image_batch(0)
    for n, batch in enumerate(batches):
        for k in range(1, ny):
            to, _ = at_y(k)
            arrived(txt_all.at[to, batch], r_ty.at[n, to])
    for n in (1, 0):
        for k in range(1, nxc):
            to, _ = at_xc(k)
            arrived(img_all.at[to, pairs_of[n]], r_ix.at[n, to])

    n_img, n_txt = nxc * na * own, ny * nb * own
    img = img_all[...].astype(F32).reshape(n_img, width).astype(BF16)
    txt = txt_all[...].astype(F32).reshape(n_txt, width).astype(BF16)
    scores = lax.dot_general(txt, img, (((1,), (1,)), ((), ())), preferred_element_type=F32)
    at_i = lax.broadcasted_iota(jnp.int32, (1, n_img), 1)
    at_t = lax.broadcasted_iota(jnp.int32, (n_txt, 1), 0)

    def stepped(steps, index):
        value = jnp.zeros_like(index)
        for i, s in enumerate(steps):
            value = jnp.where(index == i, s, value)
        return value

    i_xc, i_z = at_i // (na * own), (z + nz - stepped(img_to, (at_i // own) % na)) % nz
    t_y, t_z = at_t // (nb * own), (z + nz - stepped(txt_to, (at_t // own) % nb)) % nz
    i_row, i_col = device(i_xc // nc, y, i_xc % nc, i_z)
    t_row, t_col = device(x, t_y, core, t_z)
    rows, cols = nx * nzh * nc, ny * nzl
    i_id = (i_row * cols + i_col) * own + at_i % own
    t_id = (t_col * rows + t_row) * own + at_t % own
    same = i_id == t_id
    logits = temp * scores + offset
    margin = jnp.where(same, -logits, logits)
    e = jnp.exp(-jnp.abs(margin))
    sig = jnp.where(margin >= 0, 1.0, e) / (1.0 + e)
    dlogit = jnp.where(same, -sig, sig)
    loss = jnp.maximum(margin, 0.0) + jnp.log1p(e)

    def total(v):
        return jnp.sum(jnp.sum(v, axis=0, keepdims=True), axis=1, keepdims=True)

    lane = lax.broadcasted_iota(jnp.int32, (1, 128), 1)
    sc_z[z] = jnp.where(
        lane == 0, total(loss), jnp.where(lane == 1, total(dlogit * scores), total(dlogit))
    )
    pl.semaphore_wait(ready, 2)
    for step in sorted(range(1, nz), key=lambda s: -min(s, nz - s)):
        remote(sc_z.at[z], sc_z.at[z], s_sz, r_sz, at_z(step)).start()
    low = dlogit.astype(BF16)
    img_part = lax.dot_general(low, txt, (((0,), (0,)), ((), ())), preferred_element_type=F32)
    img_out[...] = img_part.reshape(nxc, na, own, width).astype(BF16)
    for n, pair in enumerate(pairs_of):
        for k in range(1, nxc):
            to, dev = at_xc(k)
            send(img_out.at[to, pair], img_in.at[xc, pair], s_bx.at[n, to], r_bx.at[n, xc], dev)
    txt_part = jnp.dot(low, img, preferred_element_type=F32)
    txt_out[...] = txt_part.reshape(ny, nb // 2, 2, own, width).astype(BF16)
    for n, batch in reversed(list(enumerate(batches))):
        for k in range(1, ny):
            to, dev = at_y(k)
            send(txt_out.at[to, batch], txt_in.at[y, batch], s_by.at[n, to], r_by.at[n, y], dev)

    def return_images(n):
        pair = pairs_of[n]
        acc = img_out[xc, pair].astype(F32)
        for k in range(1, nxc):
            to, _ = at_xc(k)
            arrived(img_in.at[to, pair], r_bx.at[n, to])
            acc += img_in[to, pair].astype(F32)
        img_zout[pair] = acc.astype(BF16)
        for i in (2 * n, 2 * n + 1):
            send(img_zout.at[i], img_zin.at[i], s_bi.at[i], r_bi.at[i], at_z(-img_to[i]))

    def return_texts(n):
        batch = batches[n]
        acc = txt_out[y, batch].astype(F32)
        for k in range(1, ny):
            to, _ = at_y(k)
            arrived(txt_in.at[to, batch], r_by.at[n, to])
            acc += txt_in[to, batch].astype(F32)
        txt_zout[batch] = acc.astype(BF16)
        for i in range(n * half, n * half + half):
            for j in range(2):
                at = i * 2 + j
                send(txt_zout.at[i, j], txt_zin.at[at], s_bt.at[at], r_bt.at[at], at_z(-txt_to[at]))

    return_images(0)
    return_texts(len(batches) - 1)
    return_images(1)
    for n in range(len(batches) - 1):
        return_texts(n)

    others = sc_z.at[pl.ds(0, nz - 1)]
    remote(others, others, s_sz, r_sz, at_z(1)).wait_recv()
    sc_near[q] = jnp.sum(sc_z[...], axis=0)
    for k in range(1, nq):
        to = lax.rem(q + k, nq)
        dev = device(to // (ny * nc), (to // nc) % ny, lax.rem(to, nc), z)
        remote(sc_near.at[q], sc_near.at[q], s_sn, r_sn, dev).start()

    def finish(at, gathered, sem):
        for i in range(gathered.shape[0]):
            arrived(gathered.at[i], sem.at[i])
        g = temp * jnp.sum(gathered[...].astype(F32), axis=0)
        u = unit[at]
        along = jnp.sum(u * g, axis=-1, keepdims=True)
        grads[at] = (g - u * along) / norm[at]

    finish(1, txt_zin, r_bt)
    finish(0, img_zin, r_bi)
    store = pltpu.make_async_copy(grads, grads_out, load_sem.at[4])
    store.start()

    for copy in pending:
        copy.wait_send()
    remote(others, others, s_sz, r_sz, at_z(1)).wait_send()
    rest = sc_near.at[pl.ds(0, nq - 1)]
    remote(rest, rest, s_sn, r_sn, at_z(1)).wait_send()
    remote(rest, rest, s_sn, r_sn, at_z(1)).wait_recv()
    pairs = float(rows * cols * own)
    scale = 1.0 / (pairs * pairs)
    result = jnp.sum(sc_near[...], axis=0) * scale
    terms[...] = jnp.where(lane == 1, temp, 1.0) * result
    store.wait()


def write_out(grads, terms, image_grad, text_grad, loss, slope, shift):
    image_grad[...] = grads[0]
    text_grad[...] = grads[1]
    for i, out in enumerate((loss, slope, shift)):
        out[...] = terms[:, i : i + 1]


def on_device(factors, images, texts, log_temp, bias):
    nx, nzh, nc, ny, nzl = (factors[k] for k in ("nx", "nzh", "nc", "ny", "nzl"))
    nxc, na, nn = nx * nc, sum(len(n) for n in factors["img_next"]), len(factors["txt_next"])
    nb, nw = 2 * nn, max(1, nn // (nn // 2 or 1))
    own, width = images.shape
    n_pairs = (nxc * na * own) * (ny * nb * own)
    vmem = pl.BlockSpec(memory_space=pltpu.VMEM)
    hbm = pl.BlockSpec(memory_space=pltpu.HBM)

    def low(*lead):
        return pltpu.VMEM(lead + (own, width), BF16)

    def sems(*counts):
        return [pltpu.SemaphoreType.DMA(c) for c in counts for _ in range(2)]

    grads, terms = pl.pallas_call(
        functools.partial(kernel, *factors.values()),
        out_shape=(
            jax.ShapeDtypeStruct((2, own, width), F32),
            jax.ShapeDtypeStruct((1, 128), F32),
        ),
        in_specs=[hbm] * 4,
        out_specs=(hbm, vmem),
        scratch_shapes=[
            pltpu.VMEM((2, own, width), F32),
            pltpu.VMEM((2, own, width), F32),
            pltpu.VMEM((2, own, 1), F32),
            low(), low(), low(2), low(2),
            low(nxc, na), low(ny, nn, 2),
            low(nxc, na), low(ny, nn, 2), low(nxc, na), low(ny, nn, 2),
            low(na), low(nn, 2), low(na), low(nb),
            pltpu.VMEM((nx * ny * nc, 1, 128), F32),
            pltpu.VMEM((nzh * nzl, 1, 128), F32),
            pltpu.SMEM((2, 1), F32),
            pltpu.VMEM((2, own, width), F32),
            pltpu.SemaphoreType.DMA((5,)),
        ] + sems(
            (2,), (2,), (na,), (nn,), (2, nxc), (nw, ny), (2, nxc), (nw, ny), (na,), (nb,), (), ()
        ) + [pltpu.SemaphoreType.REGULAR],
        cost_estimate=pl.CostEstimate(flops=6 * n_pairs * width, bytes_accessed=4 * own * width * 4, transcendentals=2 * n_pairs),
        compiler_params=pltpu.CompilerParams(
            collective_id=0, has_side_effects=True
        ),
    )(images, texts, log_temp, bias)
    one = jax.ShapeDtypeStruct((1, 1), F32)
    block = jax.ShapeDtypeStruct((own, width), F32)
    image_grad, text_grad, loss, slope, shift = pl.pallas_call(
        write_out,
        out_shape=(block, block, one, one, one),
        in_specs=[vmem] * 2,
        out_specs=(vmem,) * 5,
        compiler_params=pltpu.CompilerParams(),
    )(grads, terms)
    return image_grad, text_grad, loss[0, 0], slope[0, 0], shift[0, 0]


def solution(mesh, factors=FACTORS):
    in_specs = (P(("row", "col"), None), P(("col", "row"), None), P(), P())
    out_specs = (P(("row", "col"), None), P(("col", "row"), None), P(), P(), P())
    return jax.shard_map(
        functools.partial(on_device, factors),
        mesh=mesh, in_specs=in_specs, out_specs=out_specs, check_vma=False,
    )
```
